512 devices in a mesh: dp: 32 (over z, core), seq: 16 (over y, x).
Axes of the slice: x: 4, y: 4, z: 16, core: 2. Of those that a mesh axis runs over, the one named last changes fastest.
Arguments:
- query_input: bfloat16 [32, 16, 240, 1536], P('dp', 'seq'), may hold values from -8 to 8
- key_input: bfloat16 [32, 16, 240, 1536], P('dp', 'seq'), may hold values from -8 to 8
- value_input: bfloat16 [32, 16, 240, 1536], P('dp', 'seq'), may hold values from -6 to 6
- cotangent: bfloat16 [32, 16, 240, 1536], P('dp', 'seq'), may hold values from -6 to 6
- q_gain: float32 [1536], P('dp'), may hold values from 0.5 to 4
- k_gain: float32 [1536], P('dp'), may hold values from 0.5 to 4
- frames: int32 [32], P('dp'), may hold values from 8 to 16, as said below
- heights: int32 [32], P('dp'), may hold values from 7 to 15, as said below
- widths: int32 [32], P('dp'), may hold values from 8 to 16, as said below
Outputs:
- query_grad: bfloat16 [32, 16, 240, 1536], P('dp', 'seq')
- key_grad: bfloat16 [32, 16, 240, 1536], P('dp', 'seq')
- value_grad: bfloat16 [32, 16, 240, 1536], P('dp', 'seq')
- q_gain_grad: float32 [1536], P('dp')
- k_gain_grad: float32 [1536], P('dp')
The draws below stay inside these ranges and needn't reach their ends.
Inputs may be any that keep to these rules, and one draw needn't show every extreme that they name: `frames`: at least half of 16 (and 1); some clip has all 16. `heights`: at least half of 15 (and 1); some clip has all 15. `widths`: at least half of 16 (and 1); some clip has all 16.
All inputs are finite; a program needn't handle non-finite values.
Results may differ from the reference program's by a relative error of at most 0.003.
The reference program's roundings to bfloat16 on the way count: a program that leaves them out, or rounds other values in their place, can miss the bound.
Values may be sent and summed in bfloat16 or wider, within the bound.
A program may use at most 64 MiB of HBM per device.

```python
import math
import jax
import jax.numpy as jnp
from jax import lax

HEADS = 12
HEAD_DIM = 128
PATCH_ROWS = 15
PATCH_COLS = 16
CLIPS = 32
FRAMES = 16
PATCHES = 240
CHANNELS = 1536


def key_values(key):
    return jax.random.normal(jax.random.fold_in(key, 101), (CLIPS, FRAMES, PATCHES, HEADS * HEAD_DIM), jnp.float32)


def draw_key_input(key, part):
    return jnp.clip(key_values(key), -8.0, 8.0).astype(jnp.bfloat16)


def draw_query_input(key, part):
    key = jax.random.fold_in(key, 21)
    shape = (CLIPS, FRAMES, PATCHES, HEADS * HEAD_DIM)
    own = jax.random.normal(key, shape, jnp.float32)
    return jnp.clip(own, -8.0, 8.0).astype(jnp.bfloat16)


def gain_values(key):
    return jnp.exp(jax.random.uniform(key, (HEADS * HEAD_DIM,), jnp.float32, jnp.log(0.5), jnp.log(2.0)))


def draw_q_gain(key, part):
    key = jax.random.fold_in(key, 31)
    return gain_values(key)


def draw_k_gain(key, part):
    key = jax.random.fold_in(key, 41)
    return gain_values(key)


def counts_upto(key, top_value):
    low = max(1, top_value // 2)
    counts = jax.random.randint(key, (CLIPS,), low, top_value + 1)
    where_full = jax.random.randint(jax.random.fold_in(key, 5), (), 0, CLIPS)
    return counts.at[where_full].set(top_value).astype(jnp.int32)


def draw_frames(key, part):
    key = jax.random.fold_in(key, 11)
    return counts_upto(key, FRAMES)


def draw_heights(key, part):
    key = jax.random.fold_in(key, 12)
    return counts_upto(key, PATCH_ROWS)


def draw_widths(key, part):
    key = jax.random.fold_in(key, 13)
    return counts_upto(key, PATCH_COLS)


def block_levels(own_key, shape, split, least, high):
    def one(axis_at, blocks):
        steps = jax.random.uniform(jax.random.fold_in(jax.random.fold_in(own_key, 6), axis_at), (blocks,), jnp.float32, least / len(split), high / len(split))
        return jnp.repeat(jnp.exp(steps), shape[axis_at] // blocks).reshape((-1,) + (1,) * (len(shape) - axis_at - 1))

    level = one(*split[0])
    for cut in split[1:]:
        level = level * one(*cut)
    return level


def noise(stream_key, extent, spread, most, pieces=(), held_as=jnp.bfloat16):
    level = block_levels(stream_key, extent, pieces, -0.22, 0.18) if pieces else 1.0
    drawn = jax.random.normal(stream_key, extent, jnp.float32) * spread * level
    return jnp.minimum(jnp.maximum(drawn, -most), most).astype(held_as)


def setup_inputs(seed: int = 0) -> dict:
    key_of = jax.random.split(jax.random.key(seed), 10)
    return {
        "query_input": draw_query_input(jax.random.fold_in(key_of[9], 71), 0),
        "key_input": draw_key_input(jax.random.fold_in(key_of[9], 71), 0),
        "value_input": noise(key_of[2], (CLIPS, FRAMES, PATCHES, CHANNELS), 1.0, 6.0, ((0, 32), (1, 16))),
        "cotangent": noise(key_of[3], (CLIPS, FRAMES, PATCHES, CHANNELS), 1.0, 6.0, ((0, 32), (1, 16))),
        "q_gain": draw_q_gain(jax.random.fold_in(key_of[9], 71), 0),
        "k_gain": draw_k_gain(jax.random.fold_in(key_of[9], 71), 0),
        "frames": draw_frames(jax.random.fold_in(key_of[9], 71), 0),
        "heights": draw_heights(jax.random.fold_in(key_of[9], 71), 0),
        "widths": draw_widths(jax.random.fold_in(key_of[9], 71), 0),
    }


EPS = 1e-06
NEGATIVE = -1e+30

def normalize(inputs, gain):
    values = inputs.astype(jnp.float32).reshape(inputs.shape[0], inputs.shape[1], HEADS, HEAD_DIM)
    inverse = lax.rsqrt(lax.optimization_barrier(jnp.mean(values * values, axis=-1, keepdims=True)) + EPS)
    scales = gain.reshape(HEADS, HEAD_DIM)
    return ((values * inverse * scales).astype(jnp.bfloat16), values, inverse, scales)

def attend(queries, keys, values, cotan, valid, seq_first):
    if seq_first:
        score_form, out_form, back_form = ('ibhd,jbhd->bhij', 'bhij,jbhd->ibhd', 'bhij,ibhd->jbhd')
        key_mask = jnp.transpose(valid)[:, None, None, :]
    else:
        score_form, out_form, back_form = ('bihd,bjhd->bhij', 'bhij,bjhd->bihd', 'bhij,bihd->bjhd')
        key_mask = valid[:, None, None, :]
    scale = 1.0 / math.sqrt(HEAD_DIM)
    f32 = jnp.float32
    scores = jnp.einsum(score_form, queries.astype(f32), keys.astype(f32)) * scale
    scores = jnp.where(key_mask, scores, NEGATIVE)
    top = lax.optimization_barrier(jnp.max(scores, axis=-1, keepdims=True))
    expo = jnp.exp(scores - top)
    probs = expo / lax.optimization_barrier(jnp.sum(expo, axis=-1, keepdims=True))
    probs_b = probs.astype(jnp.bfloat16)
    dprobs = jnp.einsum(score_form, cotan.astype(f32), values.astype(f32))
    value_part = jnp.einsum(back_form, probs_b.astype(f32), cotan.astype(f32))
    delta = lax.optimization_barrier(jnp.sum(probs * dprobs, axis=-1, keepdims=True))
    dscores = (probs * (dprobs - delta) * scale).astype(jnp.bfloat16)
    query_part = jnp.einsum(out_form, dscores.astype(f32), keys.astype(f32))
    key_part = jnp.einsum(back_form, dscores.astype(f32), queries.astype(f32))
    return (query_part, key_part, value_part)

def rounded(values):
    return lax.optimization_barrier(values.astype(jnp.bfloat16)).astype(jnp.float32)

def unnorm(grads, values, inverse, scales):
    scaled = scales * grads
    inputs_grad = inverse * scaled - values * inverse ** 3 * lax.optimization_barrier(jnp.mean(scaled * values, axis=-1, keepdims=True))
    gain_grad = lax.optimization_barrier(jnp.sum(grads * values * inverse, axis=(0, 1)))
    return (inputs_grad, gain_grad)

def one_clip(items):
    query_input, key_input, value_input, cotangent, q_gain, k_gain, count_f, count_h, count_w = items
    spots = jnp.arange(PATCHES)
    valid = (jnp.arange(FRAMES)[:, None] < count_f) & (spots // PATCH_COLS < count_h)[None, :] & (spots % PATCH_COLS < count_w)[None, :]
    normed_q, values_q, inverse_q, scales_q = normalize(query_input, q_gain)
    normed_k, values_k, inverse_k, scales_k = normalize(key_input, k_gain)
    shape4 = (FRAMES, PATCHES, HEADS, HEAD_DIM)
    masked_cot = jnp.where(valid[:, :, None, None], cotangent.reshape(shape4), jnp.zeros((), jnp.bfloat16))
    values4 = value_input.reshape(shape4)
    sq, sk, sv = attend(normed_q, normed_k, values4, masked_cot, valid, False)
    tq, tk, tv = attend(normed_q, normed_k, values4, masked_cot, valid, True)
    grad_q = sq + rounded(tq)
    grad_k = sk + rounded(tk)
    value_grad = (sv + rounded(tv)).astype(jnp.bfloat16)
    query_grad, gain_q = unnorm(grad_q, values_q, inverse_q, scales_q)
    key_grad, gain_k = unnorm(grad_k, values_k, inverse_k, scales_k)
    full = (FRAMES, PATCHES, HEADS * HEAD_DIM)
    return (query_grad.astype(jnp.bfloat16).reshape(full), key_grad.astype(jnp.bfloat16).reshape(full), value_grad.reshape(full), gain_q.reshape(-1), gain_k.reshape(-1))

def reference(query_input, key_input, value_input, cotangent, q_gain, k_gain, frames, heights, widths):

    def run(items):
        return one_clip((items[0], items[1], items[2], items[3], q_gain, k_gain, items[4], items[5], items[6]))
    query_grad, key_grad, value_grad, gains_q, gains_k = lax.map(run, (query_input, key_input, value_input, cotangent, frames, heights, widths))
    return (query_grad, key_grad, value_grad, lax.optimization_barrier(jnp.sum(gains_q, axis=0)), lax.optimization_barrier(jnp.sum(gains_k, axis=0)))
```

```python
import functools
import math

import jax
import jax.numpy as jnp
from jax import lax
from jax.experimental import pallas as pl
from jax.experimental.pallas import tpu as pltpu
from jax.sharding import PartitionSpec as P

HEADS = 12
DIM = 128
COLS = 16
FRAMES = 16
SPOTS = 240
BLOCK = 16
CHANNELS = HEADS * DIM
EPS = 1e-06
NEGATIVE = -1e30
FAR = -2e30
SCALE = 1.0 / math.sqrt(DIM)
MESH = pl.DeviceIdType.MESH
F32 = jnp.float32
BF16 = jnp.bfloat16


def dot(a, b, dims):
    return lax.dot_general(a, b, (dims, ((), ())), preferred_element_type=F32)


def inverse_norm(values):
    return lax.rsqrt(jnp.sum(values * values, axis=-1, keepdims=True) * (1.0 / DIM) + EPS)


def attend(queries, keys, values, cotan, bias):
    scores = dot(keys, queries, ((1,), (1,))) * SCALE + bias
    top = jnp.max(scores, axis=0, keepdims=True)
    expo = jnp.exp(scores - top)
    probs = expo / jnp.sum(expo, axis=0, keepdims=True)
    dprobs = dot(values, cotan, ((1,), (1,)))
    value_part = dot(probs.astype(BF16), cotan, ((1,), (0,)))
    delta = jnp.sum(probs * dprobs, axis=0, keepdims=True)
    dscores = (probs * (dprobs - delta) * SCALE).astype(BF16)
    key_part = dot(dscores, queries, ((1,), (0,)))
    query_part = dot(dscores, keys, ((0,), (0,)))
    return query_part, key_part, value_part


def idle_of(head):
    return jnp.where(head < 11, head, 15)


def main_kernel(
    q_hbm, k_hbm, v_hbm, c_hbm, gains, frames, heights, widths,
    dq_hbm, dk_hbm, dv_hbm, gpart,
    stack, recv, tout, ret, sgrad, outs, bias_t,
    load_sem, fwd_send, fwd_recv, own_sem, back_send, back_recv, out_sem,
):
    me = lax.axis_index("seq")

    loads = [
        pltpu.make_async_copy(src, stack.at[a], load_sem.at[a])
        for a, src in enumerate((q_hbm, k_hbm, v_hbm, c_hbm))
    ]
    for load in loads:
        load.start()

    barrier = pltpu.get_barrier_semaphore()

    def greet(i, carry):
        to = lax.rem(me + i, 16)
        pl.semaphore_signal(barrier, inc=1, device_id={"seq": to}, device_id_type=MESH)
        return carry

    lax.fori_loop(1, 16, greet, 0)
    for load in loads:
        load.wait()
    pl.semaphore_wait(barrier, 15)

    def lanes(head):
        return pl.ds(pl.multiple_of(head * DIM, DIM), DIM)

    def rows(block):
        return pl.ds(pl.multiple_of(block * BLOCK, BLOCK), BLOCK)

    def send_head(head, carry):
        idle = idle_of(head)

        def send_one(i, inner):
            to = lax.rem(me + i, 16)
            block = jnp.where(to < 15, to, head)

            @pl.when(to != idle)
            def _():
                pltpu.make_async_remote_copy(
                    src_ref=stack.at[:, rows(block), lanes(head)],
                    dst_ref=recv.at[head, :, rows(me), :],
                    send_sem=fwd_send.at[head],
                    recv_sem=fwd_recv.at[head],
                    device_id={"seq": to},
                    device_id_type=MESH,
                ).start()

            return inner

        lax.fori_loop(1, 16, send_one, 0)

        @pl.when(me != idle)
        def _():
            block = jnp.where(me < 15, me, head)
            pltpu.make_async_copy(
                stack.at[:, rows(block), lanes(head)],
                recv.at[head, :, rows(me), :],
                own_sem.at[head],
            ).start()

        return carry

    lax.fori_loop(0, HEADS, send_head, 0)

    count_f, count_h, count_w = frames[0], heights[0], widths[0]

    def spot_fits(spot):
        return (spot // COLS < count_h) & (spot % COLS < count_w)

    spot = lax.broadcasted_iota(jnp.int32, (SPOTS, 1), 0)
    valid_s = spot_fits(spot) & (me < count_f)
    bias_s = jnp.where(valid_s, 0.0, NEGATIVE).astype(F32)
    cot_s = jnp.where(valid_s, 1.0, 0.0).astype(F32)

    def spatial(head, carry):
        q32 = stack[0, :, lanes(head)].astype(F32)
        k32 = stack[1, :, lanes(head)].astype(F32)
        inv_q, inv_k = inverse_norm(q32), inverse_norm(k32)
        gain_q, gain_k = gains[pl.ds(head, 1), :], gains[pl.ds(head + HEADS, 1), :]
        scaled_q, scaled_k = q32 * inv_q, k32 * inv_k
        normed_q = (scaled_q * gain_q).astype(BF16)
        normed_k = (scaled_k * gain_k).astype(BF16)
        cotan = (stack[3, :, lanes(head)].astype(F32) * cot_s).astype(BF16)
        part_q, part_k, part_v = attend(normed_q, normed_k, stack[2, :, lanes(head)], cotan, bias_s)
        sgrad[head, 0] = part_q
        sgrad[head, 1] = part_k
        sgrad[head, 2] = part_v
        gpart[pl.ds(head, 1), :] = jnp.sum(part_q * scaled_q, axis=0, keepdims=True)
        gpart[pl.ds(head + HEADS, 1), :] = jnp.sum(part_k * scaled_k, axis=0, keepdims=True)
        return carry

    lax.fori_loop(0, HEADS, spatial, 0)

    line = lax.broadcasted_iota(jnp.int32, (256, 1), 0)
    key_at = lax.broadcasted_iota(jnp.int32, (256, 256), 0)
    query_at = lax.broadcasted_iota(jnp.int32, (256, 256), 1)
    same = key_at % BLOCK == query_at % BLOCK

    def temporal(head, carry):
        idle = idle_of(head)

        @pl.when(me != idle)
        def _():
            block = jnp.where(me < 15, me, head)
            pltpu.make_async_copy(
                recv.at[head, :, pl.ds(0, 240), :], recv.at[head, :, pl.ds(0, 240), :], fwd_recv.at[head]
            ).wait()
            pltpu.make_async_copy(
                recv.at[head, :, pl.ds(0, 16), :], recv.at[head, :, pl.ds(0, 16), :], own_sem.at[head]
            ).wait()
            valid_t = spot_fits(block * BLOCK + line % BLOCK) & (line // BLOCK < count_f)
            cot_t = jnp.where(valid_t, 1.0, 0.0).astype(F32)
            bias_t[...] = jnp.where(same, jnp.where(valid_t, 0.0, NEGATIVE), FAR).astype(F32)
            q32 = recv[head, 0].astype(F32)
            k32 = recv[head, 1].astype(F32)
            inv_q, inv_k = inverse_norm(q32), inverse_norm(k32)
            gain_q, gain_k = gains[pl.ds(head, 1), :], gains[pl.ds(head + HEADS, 1), :]
            scaled_q, scaled_k = q32 * inv_q, k32 * inv_k
            normed_q = (scaled_q * gain_q).astype(BF16)
            normed_k = (scaled_k * gain_k).astype(BF16)
            cotan = (recv[head, 3].astype(F32) * cot_t).astype(BF16)
            part_q, part_k, part_v = attend(normed_q, normed_k, recv[head, 2], cotan, bias_t[...])
            part_q, part_k = part_q.astype(BF16), part_k.astype(BF16)
            tout[head, 0] = part_q
            tout[head, 1] = part_k
            tout[head, 2] = part_v.astype(BF16)

            def send_back(i, inner):
                to = lax.rem(me + i, 16)
                pltpu.make_async_remote_copy(
                    src_ref=tout.at[head, :, rows(to), :],
                    dst_ref=ret.at[head, :, rows(block), :],
                    send_sem=back_send.at[head],
                    recv_sem=back_recv.at[head],
                    device_id={"seq": to},
                    device_id_type=MESH,
                ).start()
                return inner

            lax.fori_loop(1, 16, send_back, 0)
            pltpu.make_async_copy(
                tout.at[head, :, rows(me), :], ret.at[head, :, rows(block), :], own_sem.at[head]
            ).start()
            gpart[pl.ds(head, 1), :] += jnp.sum(part_q.astype(F32) * scaled_q, axis=0, keepdims=True)
            gpart[pl.ds(head + HEADS, 1), :] += jnp.sum(
                part_k.astype(F32) * scaled_k, axis=0, keepdims=True
            )

        return carry

    lax.fori_loop(0, HEADS, temporal, 0)

    def finish(head, carry):
        idle = idle_of(head)

        @pl.when(me != idle)
        def _():
            pltpu.make_async_copy(
                ret.at[head, :, pl.ds(0, 224), :], ret.at[head, :, pl.ds(0, 224), :], back_recv.at[head]
            ).wait()
            pltpu.make_async_copy(
                ret.at[head, :, pl.ds(0, 16), :], ret.at[head, :, pl.ds(0, 16), :], own_sem.at[head]
            ).wait()

        @pl.when(me == idle)
        def _():
            pltpu.make_async_copy(ret.at[head], ret.at[head], back_recv.at[head]).wait()

        for a in range(2):
            raw = stack[a, :, lanes(head)].astype(F32)
            inverse = inverse_norm(raw)
            gain = gains[pl.ds(head + HEADS * a, 1), :]
            scaled = gain * (sgrad[head, a] + ret[head, a].astype(F32))
            mean = jnp.sum(scaled * raw, axis=-1, keepdims=True) * (1.0 / DIM)
            outs[a, :, lanes(head)] = (
                inverse * scaled - raw * (inverse * inverse * inverse) * mean
            ).astype(BF16)
        outs[2, :, lanes(head)] = (sgrad[head, 2] + ret[head, 2].astype(F32)).astype(BF16)
        for a, dst in enumerate((dq_hbm, dk_hbm, dv_hbm)):
            pltpu.make_async_copy(
                outs.at[a, :, lanes(head)], dst.at[:, lanes(head)], out_sem.at[a]
            ).start()
        return carry

    lax.fori_loop(0, HEADS, finish, 0)

    def drain(head, carry):
        idle = idle_of(head)

        @pl.when(me != idle)
        def _():
            pltpu.make_async_copy(
                recv.at[head, :, pl.ds(0, 224), :], recv.at[head, :, pl.ds(0, 224), :], fwd_send.at[head]
            ).wait()
            pltpu.make_async_copy(
                tout.at[head, :, pl.ds(0, 240), :], tout.at[head, :, pl.ds(0, 240), :], back_send.at[head]
            ).wait()

        @pl.when(me == idle)
        def _():
            pltpu.make_async_copy(
                recv.at[head, :, pl.ds(0, 240), :], recv.at[head, :, pl.ds(0, 240), :], fwd_send.at[head]
            ).wait()

        return carry

    lax.fori_loop(0, HEADS, drain, 0)
    for a, dst in enumerate((dq_hbm, dk_hbm, dv_hbm)):
        pltpu.make_async_copy(outs.at[a], dst, out_sem.at[a]).wait()


def main_call(q, k, v, c, gains, frames, heights, widths):
    any_spec = pl.BlockSpec(memory_space=pltpu.HBM)
    vmem = pl.BlockSpec(memory_space=pltpu.VMEM)
    smem = pl.BlockSpec(memory_space=pltpu.SMEM)
    grad = jax.ShapeDtypeStruct((SPOTS, CHANNELS), BF16)
    return pl.pallas_call(
        main_kernel,
        out_shape=(grad, grad, grad, jax.ShapeDtypeStruct((2 * HEADS, DIM), F32)),
        in_specs=[any_spec] * 4 + [vmem] + [smem] * 3,
        out_specs=(any_spec, any_spec, any_spec, vmem),
        scratch_shapes=[
            pltpu.VMEM((4, SPOTS, CHANNELS), BF16),
            pltpu.VMEM((HEADS, 4, 256, DIM), BF16),
            pltpu.VMEM((HEADS, 3, 256, DIM), BF16),
            pltpu.VMEM((HEADS, 3, SPOTS, DIM), BF16),
            pltpu.VMEM((HEADS, 3, SPOTS, DIM), F32),
            pltpu.VMEM((3, SPOTS, CHANNELS), BF16),
            pltpu.VMEM((256, 256), F32),
            pltpu.SemaphoreType.DMA((4,)),
            pltpu.SemaphoreType.DMA((HEADS,)),
            pltpu.SemaphoreType.DMA((HEADS,)),
            pltpu.SemaphoreType.DMA((HEADS,)),
            pltpu.SemaphoreType.DMA((HEADS,)),
            pltpu.SemaphoreType.DMA((HEADS,)),
            pltpu.SemaphoreType.DMA((3,)),
        ],
        compiler_params=pltpu.CompilerParams(
            collective_id=1, has_side_effects=True, vmem_limit_bytes=40 << 20
        ),
        name="axial",
    )(q, k, v, c, gains, frames, heights, widths)


def greet_all(barrier, axis, size):
    me = lax.axis_index(axis)

    def greet(i, carry):
        to = lax.rem(me + i, size)
        pl.semaphore_signal(barrier, inc=1, device_id={axis: to}, device_id_type=MESH)
        return carry

    lax.fori_loop(1, size, greet, 0)


def piece_of(i, count, size):
    start = i * size
    return start // DIM, start % DIM, start % DIM + size > DIM


def gather_kernel(count, size, q_ref, k_ref, gains, mine, held, send_sem, recv_sem):
    me = lax.axis_index("dp")
    barrier = pltpu.get_barrier_semaphore()
    greet_all(barrier, "dp", count)
    mine[...] = jnp.zeros_like(mine)
    mine[0:1, 0:size] = q_ref[...]
    mine[1:2, 0:size] = k_ref[...]
    mine[...] = pltpu.roll(mine[...], lax.rem(me * size, DIM), 1)
    held[me] = mine[...]
    pl.semaphore_wait(barrier, count - 1)

    def send(i, carry):
        to = lax.rem(me + i, count)
        pltpu.make_async_remote_copy(
            src_ref=mine,
            dst_ref=held.at[me],
            send_sem=send_sem,
            recv_sem=recv_sem,
            device_id={"dp": to},
            device_id_type=MESH,
        ).start()
        return carry

    lax.fori_loop(1, count, send, 0)
    others = held.at[pl.ds(0, count - 1)]
    pltpu.make_async_copy(others, others, recv_sem).wait()
    pltpu.make_async_copy(others, others, send_sem).wait()
    lane = lax.broadcasted_iota(jnp.int32, (8, DIM), 1)
    total = [jnp.zeros((8, DIM), F32) for _ in range(HEADS)]
    for i in range(count):
        head, off, spills = piece_of(i, count, size)
        tile = held[i]
        total[head] += jnp.where(lane >= off, tile, 0.0)
        if spills:
            total[head + 1] += jnp.where(lane < off, tile, 0.0)
    for head in range(HEADS):
        gains[head : head + 1, :] = total[head][0:1]
        gains[head + HEADS : head + HEADS + 1, :] = total[head][1:2]


def gather_gains(q_gain, k_gain, count):
    size = q_gain.shape[0]
    vmem = pl.BlockSpec(memory_space=pltpu.VMEM)
    return pl.pallas_call(
        functools.partial(gather_kernel, count, size),
        out_shape=jax.ShapeDtypeStruct((2 * HEADS, DIM), F32),
        in_specs=[vmem, vmem],
        out_specs=vmem,
        scratch_shapes=[
            pltpu.VMEM((8, DIM), F32),
            pltpu.VMEM((count, 8, DIM), F32),
            pltpu.SemaphoreType.DMA,
            pltpu.SemaphoreType.DMA,
        ],
        compiler_params=pltpu.CompilerParams(collective_id=2, has_side_effects=True),
        name="gather_gains",
    )(q_gain.reshape(1, size), k_gain.reshape(1, size))


def reduce_kernel(
    count, size, gpart, q_out, k_out, cut, held, mine, line, send_sem, recv_sem, send2_sem, recv2_sem
):
    me = lax.axis_index("dp")
    place = lax.axis_index("seq")
    barrier = pltpu.get_barrier_semaphore()
    greet_all(barrier, "dp", count)
    greet_all(barrier, "seq", FRAMES)
    lane = lax.broadcasted_iota(jnp.int32, (1, DIM), 1)
    cut[...] = jnp.zeros_like(cut)
    for i in range(count):
        head, off, spills = piece_of(i, count, size)
        for a in range(2):
            at = head + a * HEADS
            row = gpart[at : at + 1, :]
            if spills:
                row = jnp.where(lane >= off, row, gpart[at + 1 : at + 2, :])
            cut[i, a : a + 1, :] = row
    held[me] = cut[me]
    pl.semaphore_wait(barrier, count - 1 + FRAMES - 1)

    def send(i, carry):
        to = lax.rem(me + i, count)
        pltpu.make_async_remote_copy(
            src_ref=cut.at[to],
            dst_ref=held.at[me],
            send_sem=send_sem,
            recv_sem=recv_sem,
            device_id={"dp": to},
            device_id_type=MESH,
        ).start()
        return carry

    lax.fori_loop(1, count, send, 0)
    others = held.at[pl.ds(0, count - 1)]
    pltpu.make_async_copy(others, others, recv_sem).wait()
    mine[...] = pltpu.roll(
        jnp.sum(held[...], axis=0), lax.rem(DIM - lax.rem(me * size, DIM), DIM), 1
    )
    line[place] = mine[...]

    def share(i, carry):
        to = lax.rem(place + i, FRAMES)
        pltpu.make_async_remote_copy(
            src_ref=mine,
            dst_ref=line.at[place],
            send_sem=send2_sem,
            recv_sem=recv2_sem,
            device_id={"seq": to},
            device_id_type=MESH,
        ).start()
        return carry

    lax.fori_loop(1, FRAMES, share, 0)
    pltpu.make_async_copy(others, others, send_sem).wait()
    others2 = line.at[pl.ds(0, FRAMES - 1)]
    pltpu.make_async_copy(others2, others2, recv2_sem).wait()
    pltpu.make_async_copy(others2, others2, send2_sem).wait()
    total = jnp.sum(line[...], axis=0)
    q_out[...] = total[0:1, 0:size]
    k_out[...] = total[1:2, 0:size]


def reduce_gains(gpart, count):
    size = CHANNELS // count
    vmem = pl.BlockSpec(memory_space=pltpu.VMEM)
    share = jax.ShapeDtypeStruct((1, size), F32)
    share_q, share_k = pl.pallas_call(
        functools.partial(reduce_kernel, count, size),
        out_shape=(share, share),
        in_specs=[vmem],
        out_specs=(vmem, vmem),
        scratch_shapes=[
            pltpu.VMEM((count, 8, DIM), F32),
            pltpu.VMEM((count, 8, DIM), F32),
            pltpu.VMEM((8, DIM), F32),
            pltpu.VMEM((FRAMES, 8, DIM), F32),
            pltpu.SemaphoreType.DMA,
            pltpu.SemaphoreType.DMA,
            pltpu.SemaphoreType.DMA,
            pltpu.SemaphoreType.DMA,
        ],
        compiler_params=pltpu.CompilerParams(collective_id=3, has_side_effects=True),
        name="reduce_gains",
    )(gpart)
    return share_q.reshape(size), share_k.reshape(size)


def shards(query_input, key_input, value_input, cotangent, q_gain, k_gain, frames, heights, widths):
    count = lax.axis_size("dp")
    flat = (SPOTS, CHANNELS)
    gains = gather_gains(q_gain, k_gain, count)
    query_grad, key_grad, value_grad, gpart = main_call(
        query_input.reshape(flat),
        key_input.reshape(flat),
        value_input.reshape(flat),
        cotangent.reshape(flat),
        gains,
        frames,
        heights,
        widths,
    )
    share_q, share_k = reduce_gains(gpart, count)
    full = (1, 1, SPOTS, CHANNELS)
    return (
        query_grad.reshape(full),
        key_grad.reshape(full),
        value_grad.reshape(full),
        share_q,
        share_k,
    )


def solution(mesh):
    tokens = P("dp", "seq", None, None)
    return jax.shard_map(
        shards,
        mesh=mesh,
        in_specs=(tokens,) * 4 + (P("dp"),) * 5,
        out_specs=(tokens,) * 3 + (P("dp"),) * 2,
        check_vma=False,
    )
```

```python
import functools
import math

import jax
import jax.numpy as jnp
from jax import lax
from jax.experimental import pallas as pl
from jax.experimental.pallas import tpu as pltpu
from jax.sharding import PartitionSpec as P

HEADS = 12
DIM = 128
COLS = 16
FRAMES = 16
SPOTS = 240
BLOCK = 16
CHANNELS = HEADS * DIM
EPS = 1e-06
NEGATIVE = -1e30
FAR = -2e30
SCALE = 1.0 / math.sqrt(DIM)
MESH = pl.DeviceIdType.MESH
F32 = jnp.float32
BF16 = jnp.bfloat16


def dot(a, b, dims):
    return lax.dot_general(a, b, (dims, ((), ())), preferred_element_type=F32)


def inverse_norm(values):
    return lax.rsqrt(jnp.sum(values * values, axis=-1, keepdims=True) * (1.0 / DIM) + EPS)


def attend(queries, keys, values, cotan, bias):
    scores = dot(keys, queries, ((1,), (1,))) * SCALE + bias
    top = jnp.max(scores, axis=0, keepdims=True)
    expo = jnp.exp(scores - top)
    probs = expo / jnp.sum(expo, axis=0, keepdims=True)
    dprobs = dot(values, cotan, ((1,), (1,)))
    value_part = dot(probs.astype(BF16), cotan, ((1,), (0,)))
    delta = jnp.sum(probs * dprobs, axis=0, keepdims=True)
    dscores = (probs * (dprobs - delta) * SCALE).astype(BF16)
    key_part = dot(dscores, queries, ((1,), (0,)))
    query_part = dot(dscores, keys, ((0,), (0,)))
    return query_part, key_part, value_part


def idle_of(head):
    return jnp.where(head < 11, head, 15)


def piece_of(i, size):
    start = i * size
    return start // DIM, start % DIM, start % DIM + size > DIM


def greet_all(barrier, axis, size):
    me = lax.axis_index(axis)

    def greet(i, carry):
        to = lax.rem(me + i, size)
        pl.semaphore_signal(barrier, inc=1, device_id={axis: to}, device_id_type=MESH)
        return carry

    lax.fori_loop(1, size, greet, 0)


def main_kernel(
    count, size,
    q_hbm, k_hbm, v_hbm, c_hbm, q_gain, k_gain, frames, heights, widths,
    dq_hbm, dk_hbm, dv_hbm, share_q, share_k,
    stack, recv, tout, ret, sgrad, outs, bias_t, gains, gpart, piece, pieces, cut, cuts, sums, shares,
    load_sem, fwd_send, fwd_recv, own_sem, back_send, back_recv, out_sem, gain_sem,
):
    me = lax.axis_index("seq")
    clip = lax.axis_index("dp")

    loads = [
        pltpu.make_async_copy(src, stack.at[a], load_sem.at[a])
        for a, src in enumerate((q_hbm, k_hbm, v_hbm, c_hbm))
    ]
    for load in loads:
        load.start()

    barrier = pltpu.get_barrier_semaphore()
    greet_all(barrier, "seq", FRAMES)
    greet_all(barrier, "dp", count)

    piece[...] = jnp.zeros_like(piece)
    piece[0:1, 0:size] = q_gain[...]
    piece[1:2, 0:size] = k_gain[...]
    piece[...] = pltpu.roll(piece[...], lax.rem(clip * size, DIM), 1)
    pieces[clip] = piece[...]

    for load in loads:
        load.wait()
    pl.semaphore_wait(barrier, FRAMES - 1 + count - 1)

    def lanes(head):
        return pl.ds(pl.multiple_of(head * DIM, DIM), DIM)

    def rows(block):
        return pl.ds(pl.multiple_of(block * BLOCK, BLOCK), BLOCK)

    def send_head(head, carry):
        idle = idle_of(head)

        def send_one(i, inner):
            to = lax.rem(me + i, 16)
            block = jnp.where(to < 15, to, head)

            @pl.when(to != idle)
            def _():
                pltpu.make_async_remote_copy(
                    src_ref=stack.at[:, rows(block), lanes(head)],
                    dst_ref=recv.at[head, :, rows(me), :],
                    send_sem=fwd_send.at[head],
                    recv_sem=fwd_recv.at[head],
                    device_id={"seq": to},
                    device_id_type=MESH,
                ).start()

            return inner

        lax.fori_loop(1, 16, send_one, 0)

        @pl.when(me != idle)
        def _():
            block = jnp.where(me < 15, me, head)
            pltpu.make_async_copy(
                stack.at[:, rows(block), lanes(head)],
                recv.at[head, :, rows(me), :],
                own_sem.at[head],
            ).start()

        return carry

    lax.fori_loop(0, 2, send_head, 0)

    def send_piece(i, carry):
        pltpu.make_async_remote_copy(
            src_ref=piece,
            dst_ref=pieces.at[clip],
            send_sem=gain_sem.at[0],
            recv_sem=gain_sem.at[1],
            device_id={"dp": lax.rem(clip + i, count)},
            device_id_type=MESH,
        ).start()
        return carry

    lax.fori_loop(1, count, send_piece, 0)
    lax.fori_loop(2, HEADS, send_head, 0)

    others = pieces.at[pl.ds(0, count - 1)]
    pltpu.make_async_copy(others, others, gain_sem.at[1]).wait()
    lane = lax.broadcasted_iota(jnp.int32, (8, DIM), 1)
    total = [jnp.zeros((8, DIM), F32) for _ in range(HEADS)]
    for i in range(count):
        at, off, spills = piece_of(i, size)
        tile = pieces[i]
        total[at] += jnp.where(lane >= off, tile, 0.0)
        if spills:
            total[at + 1] += jnp.where(lane < off, tile, 0.0)
    for at in range(HEADS):
        gains[at : at + 1, :] = total[at][0:1]
        gains[at + HEADS : at + HEADS + 1, :] = total[at][1:2]

    count_f, count_h, count_w = frames[0], heights[0], widths[0]

    def spot_fits(spot):
        return (spot // COLS < count_h) & (spot % COLS < count_w)

    spot = lax.broadcasted_iota(jnp.int32, (SPOTS, 1), 0)
    valid_s = spot_fits(spot) & (me < count_f)
    bias_s = jnp.where(valid_s, 0.0, NEGATIVE).astype(F32)
    cot_s = jnp.where(valid_s, 1.0, 0.0).astype(F32)

    def spatial(head, carry):
        q32 = stack[0, :, lanes(head)].astype(F32)
        k32 = stack[1, :, lanes(head)].astype(F32)
        inv_q, inv_k = inverse_norm(q32), inverse_norm(k32)
        gain_q, gain_k = gains[pl.ds(head, 1), :], gains[pl.ds(head + HEADS, 1), :]
        scaled_q, scaled_k = q32 * inv_q, k32 * inv_k
        normed_q = (scaled_q * gain_q).astype(BF16)
        normed_k = (scaled_k * gain_k).astype(BF16)
        cotan = (stack[3, :, lanes(head)].astype(F32) * cot_s).astype(BF16)
        part_q, part_k, part_v = attend(normed_q, normed_k, stack[2, :, lanes(head)], cotan, bias_s)
        sgrad[head, 0] = part_q
        sgrad[head, 1] = part_k
        sgrad[head, 2] = part_v
        gpart[pl.ds(head, 1), :] = jnp.sum(part_q * scaled_q, axis=0, keepdims=True)
        gpart[pl.ds(head + HEADS, 1), :] = jnp.sum(part_k * scaled_k, axis=0, keepdims=True)
        return carry

    lax.fori_loop(0, HEADS, spatial, 0)

    line = lax.broadcasted_iota(jnp.int32, (256, 1), 0)
    key_at = lax.broadcasted_iota(jnp.int32, (256, 256), 0)
    query_at = lax.broadcasted_iota(jnp.int32, (256, 256), 1)
    same = key_at % BLOCK == query_at % BLOCK

    def temporal(head, carry):
        idle = idle_of(head)

        @pl.when(me != idle)
        def _():
            block = jnp.where(me < 15, me, head)
            pltpu.make_async_copy(
                recv.at[head, :, pl.ds(0, 240), :], recv.at[head, :, pl.ds(0, 240), :], fwd_recv.at[head]
            ).wait()
            pltpu.make_async_copy(
                recv.at[head, :, pl.ds(0, 16), :], recv.at[head, :, pl.ds(0, 16), :], own_sem.at[head]
            ).wait()
            valid_t = spot_fits(block * BLOCK + line % BLOCK) & (line // BLOCK < count_f)
            cot_t = jnp.where(valid_t, 1.0, 0.0).astype(F32)
            bias_t[...] = jnp.where(same, jnp.where(valid_t, 0.0, NEGATIVE), FAR).astype(F32)
            q32 = recv[head, 0].astype(F32)
            k32 = recv[head, 1].astype(F32)
            inv_q, inv_k = inverse_norm(q32), inverse_norm(k32)
            gain_q, gain_k = gains[pl.ds(head, 1), :], gains[pl.ds(head + HEADS, 1), :]
            scaled_q, scaled_k = q32 * inv_q, k32 * inv_k
            normed_q = (scaled_q * gain_q).astype(BF16)
            normed_k = (scaled_k * gain_k).astype(BF16)
            cotan = (recv[head, 3].astype(F32) * cot_t).astype(BF16)
            part_q, part_k, part_v = attend(normed_q, normed_k, recv[head, 2], cotan, bias_t[...])
            part_q, part_k = part_q.astype(BF16), part_k.astype(BF16)
            tout[head, 0] = part_q
            tout[head, 1] = part_k
            tout[head, 2] = part_v.astype(BF16)

            def send_back(i, inner):
                to = lax.rem(me + i, 16)
                pltpu.make_async_remote_copy(
                    src_ref=tout.at[head, :, rows(to), :],
                    dst_ref=ret.at[head, :, rows(block), :],
                    send_sem=back_send.at[head],
                    recv_sem=back_recv.at[head],
                    device_id={"seq": to},
                    device_id_type=MESH,
                ).start()
                return inner

            lax.fori_loop(1, 16, send_back, 0)
            pltpu.make_async_copy(
                tout.at[head, :, rows(me), :], ret.at[head, :, rows(block), :], own_sem.at[head]
            ).start()
            gpart[pl.ds(head, 1), :] += jnp.sum(part_q.astype(F32) * scaled_q, axis=0, keepdims=True)
            gpart[pl.ds(head + HEADS, 1), :] += jnp.sum(
                part_k.astype(F32) * scaled_k, axis=0, keepdims=True
            )

        return carry

    lax.fori_loop(0, HEADS, temporal, 0)

    cut[...] = jnp.zeros_like(cut)
    for i in range(count):
        at, off, spills = piece_of(i, size)
        for a in range(2):
            row = gpart[at + a * HEADS : at + a * HEADS + 1, :]
            if spills:
                row = jnp.where(
                    lane[0:1] >= off, row, gpart[at + a * HEADS + 1 : at + a * HEADS + 2, :]
                )
            cut[i, a : a + 1, :] = row
    cuts[clip] = cut[clip]

    def send_cut(i, carry):
        to = lax.rem(clip + i, count)
        pltpu.make_async_remote_copy(
            src_ref=cut.at[to],
            dst_ref=cuts.at[clip],
            send_sem=gain_sem.at[2],
            recv_sem=gain_sem.at[3],
            device_id={"dp": to},
            device_id_type=MESH,
        ).start()
        return carry

    lax.fori_loop(1, count, send_cut, 0)

    def finish(head, carry):
        idle = idle_of(head)

        @pl.when(me != idle)
        def _():
            pltpu.make_async_copy(
                ret.at[head, :, pl.ds(0, 224), :], ret.at[head, :, pl.ds(0, 224), :], back_recv.at[head]
            ).wait()
            pltpu.make_async_copy(
                ret.at[head, :, pl.ds(0, 16), :], ret.at[head, :, pl.ds(0, 16), :], own_sem.at[head]
            ).wait()

        @pl.when(me == idle)
        def _():
            pltpu.make_async_copy(ret.at[head], ret.at[head], back_recv.at[head]).wait()

        for a in range(2):
            raw = stack[a, :, lanes(head)].astype(F32)
            inverse = inverse_norm(raw)
            gain = gains[pl.ds(head + HEADS * a, 1), :]
            scaled = gain * (sgrad[head, a] + ret[head, a].astype(F32))
            mean = jnp.sum(scaled * raw, axis=-1, keepdims=True) * (1.0 / DIM)
            outs[a, :, lanes(head)] = (
                inverse * scaled - raw * (inverse * inverse * inverse) * mean
            ).astype(BF16)
        outs[2, :, lanes(head)] = (sgrad[head, 2] + ret[head, 2].astype(F32)).astype(BF16)
        for a, dst in enumerate((dq_hbm, dk_hbm, dv_hbm)):
            pltpu.make_async_copy(
                outs.at[a, :, lanes(head)], dst.at[:, lanes(head)], out_sem.at[a]
            ).start()
        return carry

    lax.fori_loop(0, HEADS // 2, finish, 0)

    others = cuts.at[pl.ds(0, count - 1)]
    pltpu.make_async_copy(others, others, gain_sem.at[3]).wait()
    sums[...] = pltpu.roll(
        jnp.sum(cuts[...], axis=0), lax.rem(DIM - lax.rem(clip * size, DIM), DIM), 1
    )
    shares[me] = sums[...]

    def send_sums(i, carry):
        pltpu.make_async_remote_copy(
            src_ref=sums,
            dst_ref=shares.at[me],
            send_sem=gain_sem.at[4],
            recv_sem=gain_sem.at[5],
            device_id={"seq": lax.rem(me + i, FRAMES)},
            device_id_type=MESH,
        ).start()
        return carry

    lax.fori_loop(1, FRAMES, send_sums, 0)

    lax.fori_loop(HEADS // 2, HEADS, finish, 0)

    others = shares.at[pl.ds(0, FRAMES - 1)]
    pltpu.make_async_copy(others, others, gain_sem.at[5]).wait()
    summed = jnp.sum(shares[...], axis=0)
    share_q[...] = summed[0:1, 0:size]
    share_k[...] = summed[1:2, 0:size]

    def drain(head, carry):
        idle = idle_of(head)

        @pl.when(me != idle)
        def _():
            pltpu.make_async_copy(
                recv.at[head, :, pl.ds(0, 224), :], recv.at[head, :, pl.ds(0, 224), :], fwd_send.at[head]
            ).wait()
            pltpu.make_async_copy(
                tout.at[head, :, pl.ds(0, 240), :], tout.at[head, :, pl.ds(0, 240), :], back_send.at[head]
            ).wait()

        @pl.when(me == idle)
        def _():
            pltpu.make_async_copy(
                recv.at[head, :, pl.ds(0, 240), :], recv.at[head, :, pl.ds(0, 240), :], fwd_send.at[head]
            ).wait()

        return carry

    lax.fori_loop(0, HEADS, drain, 0)
    others = cuts.at[pl.ds(0, count - 1)]
    pltpu.make_async_copy(others, others, gain_sem.at[0]).wait()
    pltpu.make_async_copy(others, others, gain_sem.at[2]).wait()
    others = shares.at[pl.ds(0, FRAMES - 1)]
    pltpu.make_async_copy(others, others, gain_sem.at[4]).wait()
    for a, dst in enumerate((dq_hbm, dk_hbm, dv_hbm)):
        pltpu.make_async_copy(outs.at[a], dst, out_sem.at[a]).wait()


def main_call(q, k, v, c, q_gain, k_gain, frames, heights, widths, count):
    size = q_gain.shape[0]
    any_spec = pl.BlockSpec(memory_space=pl.ANY)
    vmem = pl.BlockSpec(memory_space=pltpu.VMEM)
    smem = pl.BlockSpec(memory_space=pltpu.SMEM)
    grad = jax.ShapeDtypeStruct((SPOTS, CHANNELS), BF16)
    share = jax.ShapeDtypeStruct((1, size), F32)
    arrays = [pltpu.with_memory_space_constraint(x, pltpu.HBM) for x in (q, k, v, c)]
    return pl.pallas_call(
        functools.partial(main_kernel, count, size),
        out_shape=(grad, grad, grad, share, share),
        in_specs=[any_spec] * 4 + [vmem] * 2 + [smem] * 3,
        out_specs=(any_spec, any_spec, any_spec, vmem, vmem),
        scratch_shapes=[
            pltpu.VMEM((4, SPOTS, CHANNELS), BF16),
            pltpu.VMEM((HEADS, 4, 256, DIM), BF16),
            pltpu.VMEM((HEADS, 3, 256, DIM), BF16),
            pltpu.VMEM((HEADS, 3, SPOTS, DIM), BF16),
            pltpu.VMEM((HEADS, 3, SPOTS, DIM), F32),
            pltpu.VMEM((3, SPOTS, CHANNELS), BF16),
            pltpu.VMEM((256, 256), F32),
            pltpu.VMEM((2 * HEADS, DIM), F32),
            pltpu.VMEM((2 * HEADS, DIM), F32),
            pltpu.VMEM((8, DIM), F32),
            pltpu.VMEM((count, 8, DIM), F32),
            pltpu.VMEM((count, 8, DIM), F32),
            pltpu.VMEM((count, 8, DIM), F32),
            pltpu.VMEM((8, DIM), F32),
            pltpu.VMEM((FRAMES, 8, DIM), F32),
            pltpu.SemaphoreType.DMA((4,)),
            pltpu.SemaphoreType.DMA((HEADS,)),
            pltpu.SemaphoreType.DMA((HEADS,)),
            pltpu.SemaphoreType.DMA((HEADS,)),
            pltpu.SemaphoreType.DMA((HEADS,)),
            pltpu.SemaphoreType.DMA((HEADS,)),
            pltpu.SemaphoreType.DMA((3,)),
            pltpu.SemaphoreType.DMA((6,)),
        ],
        compiler_params=pltpu.CompilerParams(
            collective_id=1, has_side_effects=True, vmem_limit_bytes=40 << 20
        ),
        name="axial",
    )(*arrays, q_gain.reshape(1, size), k_gain.reshape(1, size), frames, heights, widths)


def emit_kernel(*refs):
    half = len(refs) // 2
    sem = refs[-1]
    copies = [
        pltpu.make_async_copy(src, dst, sem.at[i])
        for i, (src, dst) in enumerate(zip(refs[:half], refs[half:-1]))
    ]
    for copy in copies:
        copy.start()
    for copy in copies:
        copy.wait()


def emit(arrays):
    any_spec = pl.BlockSpec(memory_space=pl.ANY)
    vmem = pl.BlockSpec(memory_space=pltpu.VMEM)
    return pl.pallas_call(
        emit_kernel,
        out_shape=tuple(jax.ShapeDtypeStruct(x.shape, x.dtype) for x in arrays),
        in_specs=[vmem] * len(arrays),
        out_specs=(any_spec,) * len(arrays),
        scratch_shapes=[pltpu.SemaphoreType.DMA((len(arrays),))],
        compiler_params=pltpu.CompilerParams(vmem_limit_bytes=8 << 20),
        name="emit",
    )(*arrays)


def shards(query_input, key_input, value_input, cotangent, q_gain, k_gain, frames, heights, widths):
    count = lax.axis_size("dp")
    flat = (SPOTS, CHANNELS)
    results = main_call(
        query_input.reshape(flat),
        key_input.reshape(flat),
        value_input.reshape(flat),
        cotangent.reshape(flat),
        q_gain,
        k_gain,
        frames,
        heights,
        widths,
        count,
    )
    query_grad, key_grad, value_grad, share_q, share_k = emit(results)
    full = (1, 1, SPOTS, CHANNELS)
    return (
        query_grad.reshape(full),
        key_grad.reshape(full),
        value_grad.reshape(full),
        share_q.reshape(-1),
        share_k.reshape(-1),
    )


def solution(mesh):
    tokens = P("dp", "seq", None, None)
    return jax.shard_map(
        shards,
        mesh=mesh,
        in_specs=(tokens,) * 4 + (P("dp"),) * 5,
        out_specs=(tokens,) * 3 + (P("dp"),) * 2,
        check_vma=False,
    )
```

```python
import functools
import math

import jax
import jax.numpy as jnp
from jax import lax
from jax.experimental import pallas as pl
from jax.experimental.pallas import tpu as pltpu
from jax.sharding import PartitionSpec as P

HEADS = 12
DIM = 128
COLS = 16
FRAMES = 16
SPOTS = 240
BLOCK = 16
CHANNELS = HEADS * DIM
AHEAD = 5
AHEAD2 = 2
EARLY = 8
PAIR_S = 2
PAIR_T = 2
DOWN = 0
EPS = 1e-06
NEGATIVE = -1e30
FAR = -2e30
SCALE = 1.0 / math.sqrt(DIM)
LOG2E = math.log2(math.e)
MESH = pl.DeviceIdType.MESH
F32 = jnp.float32
BF16 = jnp.bfloat16


def dot(a, b, dims):
    return lax.dot_general(a, b, (dims, ((), ())), preferred_element_type=F32)


def inverse_norm(values):
    return lax.rsqrt(jnp.sum(values * values, axis=-1, keepdims=True) * (1.0 / DIM) + EPS)


def attend(queries, keys, values, cotan, bias):
    scores = dot(keys, queries, ((1,), (1,))) * (SCALE * LOG2E) + bias
    dprobs = dot(values, cotan, ((1,), (1,)))
    expo = jnp.exp2(scores - jnp.max(scores, axis=0, keepdims=True))
    probs = expo * (1.0 / jnp.sum(expo, axis=0, keepdims=True))
    value_part = dot(probs.astype(BF16), cotan, ((1,), (0,)))
    delta = jnp.sum(probs * dprobs, axis=0, keepdims=True)
    dscores = (probs * (dprobs - delta) * SCALE).astype(BF16)
    key_part = dot(dscores, queries, ((1,), (0,)))
    query_part = dot(dscores, keys, ((0,), (0,)))
    return query_part, key_part, value_part


def partner(me, i):
    if DOWN:
        return 16 - i - jnp.where(16 - i <= me, 1, 0)
    return i - 1 + jnp.where(i > me, 1, 0)


def idle_of(head):
    return jnp.where(head < 11, head, 15)


def piece_of(i, size):
    start = i * size
    return start // DIM, start % DIM, start % DIM + size > DIM


def lead_of(place, count):
    return lax.rem(place + count // 2, count)


def main_kernel(
    count, size,
    q_hbm, k_hbm, v_hbm, c_hbm, q_gain, k_gain, frames, heights, widths,
    dq_hbm, dk_hbm, dv_hbm, share_q, share_k,
    stack, recv, tout, ret, sgrad, outs, bias_t, gains, gpart, piece, spare, pieces, cut, cuts, sums, shares,
    gain_rows, met_sem, small_sem, load_sem, fwd_send, fwd_recv, own_sem, back_send, back_recv, out_sem, gain_sem,
):
    me = lax.axis_index("seq")
    clip = lax.axis_index("dp")

    leads = clip == lead_of(me, count)

    loads = [
        pltpu.make_async_copy(src, stack.at[a], load_sem.at[a])
        for a, src in enumerate((q_hbm, k_hbm, v_hbm, c_hbm))
    ]
    smalls = [
        pltpu.make_async_copy(src, dst, small_sem.at[a])
        for a, (src, dst) in enumerate(
            ((q_gain, gain_rows.at[0]), (k_gain, gain_rows.at[1]))
        )
    ]
    barrier = pltpu.get_barrier_semaphore()

    def greet(i, carry):
        to = lax.rem(me + i, FRAMES)

        @pl.when(clip != lead_of(to, count))
        def _():
            pl.semaphore_signal(barrier, inc=1, device_id={"seq": to}, device_id_type=MESH)

        return carry

    lax.fori_loop(1, FRAMES, greet, 0)
    for load in loads:
        load.start()
    for small in smalls:
        small.start()

    @pl.when(jnp.logical_not(leads))
    def _():
        pl.semaphore_signal(
            barrier, inc=1, device_id={"dp": lead_of(me, count)}, device_id_type=MESH
        )

    for load in loads:
        load.wait()

    @pl.when(jnp.logical_not(leads))
    def _():
        pl.semaphore_wait(barrier, FRAMES - 1)

    mate = lax.rem(me + FRAMES - 1, FRAMES)

    @pl.when(clip == lead_of(mate, count))
    def _():
        pl.semaphore_signal(met_sem.at[0], inc=1, device_id={"seq": mate}, device_id_type=MESH)

    @pl.when(leads)
    def _():
        pl.semaphore_wait(met_sem.at[0], 1)

    def lanes(head):
        return pl.ds(pl.multiple_of(head * DIM, DIM), DIM)

    def rows(block):
        return pl.ds(pl.multiple_of(block * BLOCK, BLOCK), BLOCK)

    def send_head(head, carry):
        idle = idle_of(head)

        def send_one(i, inner):
            to = partner(me, i)
            block = jnp.where(to < 15, to, head)

            @pl.when(to != idle)
            def _():
                pltpu.make_async_remote_copy(
                    src_ref=stack.at[:, rows(block), lanes(head)],
                    dst_ref=recv.at[head, :, rows(me), :],
                    send_sem=fwd_send.at[head],
                    recv_sem=fwd_recv.at[head],
                    device_id={"seq": to},
                    device_id_type=MESH,
                ).start()

            return inner

        lax.fori_loop(1, 16, send_one, 0)

        @pl.when(me != idle)
        def _():
            block = jnp.where(me < 15, me, head)
            pltpu.make_async_copy(
                stack.at[:, rows(block), lanes(head)],
                recv.at[head, :, rows(me), :],
                own_sem.at[head],
            ).start()

        return carry

    ahead = jnp.where(clip < count // 2, AHEAD, AHEAD2)
    lax.fori_loop(0, ahead, send_head, 0)

    for small in smalls:
        small.wait()
    shift = lax.rem(clip * size, DIM)
    piece[...] = jnp.zeros_like(piece)
    spare[...] = jnp.zeros_like(spare)
    piece[0:1, 0:size] = gain_rows[0]
    spare[0:1, 0:size] = gain_rows[1]
    piece[...] = pltpu.roll(piece[...] + pltpu.roll(spare[...], DIM // 2, 1), shift, 1)
    pieces[clip, 0:1] = piece[0:1]

    @pl.when(leads)
    def _():
        pl.semaphore_wait(barrier, count - 1)

        def tell(i, carry):
            to = lax.rem(clip + i, count)
            pl.semaphore_signal(met_sem.at[1], inc=1, device_id={"dp": to}, device_id_type=MESH)
            return carry

        lax.fori_loop(1, count, tell, 0)

    @pl.when(jnp.logical_not(leads))
    def _():
        pl.semaphore_wait(met_sem.at[1], 1)

    def send_piece(i, carry):
        pltpu.make_async_remote_copy(
            src_ref=piece.at[pl.ds(0, 1)],
            dst_ref=pieces.at[clip, pl.ds(0, 1)],
            send_sem=gain_sem.at[0],
            recv_sem=gain_sem.at[1],
            device_id={"dp": lax.rem(clip + i, count)},
            device_id_type=MESH,
        ).start()
        return carry

    lax.fori_loop(1, count, send_piece, 0)
    lax.fori_loop(ahead, HEADS, send_head, 0)

    others = pieces.at[pl.ds(0, count - 1), pl.ds(0, 1)]
    pltpu.make_async_copy(others, others, gain_sem.at[1]).wait()
    lane = lax.broadcasted_iota(jnp.int32, (1, DIM), 1)
    total = [jnp.zeros((1, DIM), F32) for _ in range(2 * HEADS)]
    for i in range(count):
        at, off, spills = piece_of(i, size)
        row = pieces[i, 0:1]
        for a in range(2):
            if a:
                row = pltpu.roll(row, DIM // 2, 1)
            total[at + a * HEADS] += jnp.where((lane >= off) & (lane < off + size), row, 0.0)
            if spills:
                total[at + 1 + a * HEADS] += jnp.where(lane < off + size - DIM, row, 0.0)
    for at in range(2 * HEADS):
        gains[at : at + 1, :] = total[at]

    count_f, count_h, count_w = frames[0], heights[0], widths[0]

    def spot_fits(spot):
        return (spot // COLS < count_h) & (spot % COLS < count_w)

    spot = lax.broadcasted_iota(jnp.int32, (SPOTS, 1), 0)
    valid_s = spot_fits(spot) & (me < count_f)
    bias_s = jnp.where(valid_s, 0.0, NEGATIVE).astype(F32)
    cot_s = jnp.where(valid_s, 1.0, 0.0).astype(BF16)

    def spatial_head(head):
        q32 = stack[0, :, lanes(head)].astype(F32)
        k32 = stack[1, :, lanes(head)].astype(F32)
        gain_q, gain_k = gains[pl.ds(head, 1), :], gains[pl.ds(head + HEADS, 1), :]
        scaled_q, scaled_k = q32 * inverse_norm(q32), k32 * inverse_norm(k32)
        normed_q = (scaled_q * gain_q).astype(BF16)
        normed_k = (scaled_k * gain_k).astype(BF16)
        cotan = stack[3, :, lanes(head)] * cot_s
        part_q, part_k, part_v = attend(normed_q, normed_k, stack[2, :, lanes(head)], cotan, bias_s)
        sgrad[head, 0] = part_q
        sgrad[head, 1] = part_k
        sgrad[head, 2] = part_v
        gpart[pl.ds(head, 1), :] = jnp.sum(part_q * scaled_q, axis=0, keepdims=True)
        gpart[pl.ds(head + HEADS, 1), :] = jnp.sum(part_k * scaled_k, axis=0, keepdims=True)

    def spatial(step, carry):
        for j in range(PAIR_S):
            spatial_head(step * PAIR_S + j)
        return carry

    lax.fori_loop(0, HEADS // PAIR_S, spatial, 0)

    line = lax.broadcasted_iota(jnp.int32, (256, 1), 0)
    key_at = lax.broadcasted_iota(jnp.int32, (256, 256), 0)
    query_at = lax.broadcasted_iota(jnp.int32, (256, 256), 1)
    bias_t[...] = jnp.where(key_at % BLOCK == query_at % BLOCK, 0.0, FAR).astype(F32)

    units = jnp.where((me >= 11) & (me < 15), 12, 11)

    def head_of(unit):
        return unit + jnp.where((me < 11) & (unit >= me), 1, 0)

    def send_back(unit, carry):
        head = head_of(unit)
        block = jnp.where(me < 15, me, head)

        def send_one(i, inner):
            to = partner(me, i)
            pltpu.make_async_remote_copy(
                src_ref=tout.at[head, :, rows(to), :],
                dst_ref=ret.at[head, :, rows(block), :],
                send_sem=back_send.at[head],
                recv_sem=back_recv.at[head],
                device_id={"seq": to},
                device_id_type=MESH,
            ).start()
            return inner

        lax.fori_loop(1, 16, send_one, 0)
        pltpu.make_async_copy(
            tout.at[head, :, rows(me), :], ret.at[head, :, rows(block), :], own_sem.at[head]
        ).start()
        return carry

    def arrive(head):
        whole, own = recv.at[head, :, pl.ds(0, 240), :], recv.at[head, :, pl.ds(0, 16), :]
        pltpu.make_async_copy(whole, whole, fwd_recv.at[head]).wait()
        pltpu.make_async_copy(own, own, own_sem.at[head]).wait()

    def temporal_head(head):
        block = jnp.where(me < 15, me, head)
        valid_t = spot_fits(block * BLOCK + line % BLOCK) & (line // BLOCK < count_f)
        bias = bias_t[...] + jnp.where(valid_t, 0.0, NEGATIVE).astype(F32)
        q32 = recv[head, 0].astype(F32)
        k32 = recv[head, 1].astype(F32)
        gain_q, gain_k = gains[pl.ds(head, 1), :], gains[pl.ds(head + HEADS, 1), :]
        scaled_q, scaled_k = q32 * inverse_norm(q32), k32 * inverse_norm(k32)
        normed_q = (scaled_q * gain_q).astype(BF16)
        normed_k = (scaled_k * gain_k).astype(BF16)
        cotan = recv[head, 3] * jnp.where(valid_t, 1.0, 0.0).astype(BF16)
        part_q, part_k, part_v = attend(normed_q, normed_k, recv[head, 2], cotan, bias)
        part_q, part_k = part_q.astype(BF16), part_k.astype(BF16)
        tout[head, 0] = part_q
        tout[head, 1] = part_k
        tout[head, 2] = part_v.astype(BF16)
        gpart[pl.ds(head, 1), :] += jnp.sum(part_q.astype(F32) * scaled_q, axis=0, keepdims=True)
        gpart[pl.ds(head + HEADS, 1), :] += jnp.sum(
            part_k.astype(F32) * scaled_k, axis=0, keepdims=True
        )

    def temporal(step, carry):
        heads = [head_of(step * PAIR_T + j) for j in range(PAIR_T)]
        for head in heads:
            arrive(head)
        for head in heads:
            temporal_head(head)
        return carry

    def temporal_and_back(unit, carry):
        arrive(head_of(unit))
        temporal_head(head_of(unit))
        return send_back(unit, carry)

    lax.fori_loop(0, EARLY, temporal_and_back, 0)
    lax.fori_loop(EARLY // PAIR_T, 10 // PAIR_T, temporal, 0)
    arrive(head_of(10))
    temporal_head(head_of(10))

    @pl.when((me >= 11) & (me < 15))
    def _():
        arrive(11)
        temporal_head(11)

    for i in range(count):
        at, off, spills = piece_of(i, size)
        parts = []
        for a in range(2):
            row = gpart[at + a * HEADS : at + a * HEADS + 1, :]
            if spills:
                row = jnp.where(lane >= off, row, gpart[at + a * HEADS + 1 : at + a * HEADS + 2, :])
            parts.append(row)
        inside = (lane >= off) & (lane < off + size) | (lane < off + size - DIM)
        cut[i, 0:1, :] = jnp.where(inside, parts[0], pltpu.roll(parts[1], DIM // 2, 1))
    cuts[clip, 0:1] = cut[clip, 0:1]

    def send_cut(i, carry):
        to = lax.rem(clip + i, count)
        pltpu.make_async_remote_copy(
            src_ref=cut.at[to, pl.ds(0, 1)],
            dst_ref=cuts.at[clip, pl.ds(0, 1)],
            send_sem=gain_sem.at[2],
            recv_sem=gain_sem.at[3],
            device_id={"dp": to},
            device_id_type=MESH,
        ).start()
        return carry

    lax.fori_loop(1, count, send_cut, 0)
    lax.fori_loop(EARLY, units, send_back, 0)

    def finish(head, carry):
        idle = idle_of(head)

        @pl.when(me != idle)
        def _():
            pltpu.make_async_copy(
                ret.at[head, :, pl.ds(0, 224), :], ret.at[head, :, pl.ds(0, 224), :], back_recv.at[head]
            ).wait()
            pltpu.make_async_copy(
                ret.at[head, :, pl.ds(0, 16), :], ret.at[head, :, pl.ds(0, 16), :], own_sem.at[head]
            ).wait()

        @pl.when(me == idle)
        def _():
            pltpu.make_async_copy(ret.at[head], ret.at[head], back_recv.at[head]).wait()

        for a in range(2):
            raw = stack[a, :, lanes(head)].astype(F32)
            inverse = inverse_norm(raw)
            gain = gains[pl.ds(head + HEADS * a, 1), :]
            scaled = gain * (sgrad[head, a] + ret[head, a].astype(F32))
            mean = jnp.sum(scaled * raw, axis=-1, keepdims=True) * (1.0 / DIM)
            outs[a, :, lanes(head)] = (
                inverse * scaled - raw * (inverse * inverse * inverse) * mean
            ).astype(BF16)
        outs[2, :, lanes(head)] = (sgrad[head, 2] + ret[head, 2].astype(F32)).astype(BF16)
        for a, dst in enumerate((dq_hbm, dk_hbm, dv_hbm)):
            pltpu.make_async_copy(
                outs.at[a, :, lanes(head)], dst.at[:, lanes(head)], out_sem.at[a]
            ).start()
        return carry

    others = cuts.at[pl.ds(0, count - 1), pl.ds(0, 1)]
    pltpu.make_async_copy(others, others, gain_sem.at[3]).wait()
    summed = jnp.broadcast_to(jnp.sum(cuts[:, 0:1], axis=0), (8, DIM))
    sums[...] = pltpu.roll(summed, lax.rem(DIM - shift, DIM), 1)
    shares[me, 0:1] = sums[0:1]

    def send_sums(i, carry):
        pltpu.make_async_remote_copy(
            src_ref=sums.at[pl.ds(0, 1)],
            dst_ref=shares.at[me, pl.ds(0, 1)],
            send_sem=gain_sem.at[4],
            recv_sem=gain_sem.at[5],
            device_id={"seq": lax.rem(me + i, FRAMES)},
            device_id_type=MESH,
        ).start()
        return carry

    lax.fori_loop(1, FRAMES, send_sums, 0)

    lax.fori_loop(0, HEADS, finish, 0)

    others = shares.at[pl.ds(0, FRAMES - 1), pl.ds(0, 1)]
    pltpu.make_async_copy(others, others, gain_sem.at[5]).wait()
    summed = jnp.sum(shares[:, 0:1], axis=0)
    share_q[...] = summed[:, 0:size]
    share_k[...] = pltpu.roll(summed, DIM // 2, 1)[:, 0:size]

    def drain(head, carry):
        idle = idle_of(head)

        @pl.when(me != idle)
        def _():
            pltpu.make_async_copy(
                recv.at[head, :, pl.ds(0, 224), :], recv.at[head, :, pl.ds(0, 224), :], fwd_send.at[head]
            ).wait()
            pltpu.make_async_copy(
                tout.at[head, :, pl.ds(0, 240), :], tout.at[head, :, pl.ds(0, 240), :], back_send.at[head]
            ).wait()

        @pl.when(me == idle)
        def _():
            pltpu.make_async_copy(
                recv.at[head, :, pl.ds(0, 240), :], recv.at[head, :, pl.ds(0, 240), :], fwd_send.at[head]
            ).wait()

        return carry

    lax.fori_loop(0, HEADS, drain, 0)
    others = cuts.at[pl.ds(0, count - 1), pl.ds(0, 1)]
    pltpu.make_async_copy(others, others, gain_sem.at[0]).wait()
    pltpu.make_async_copy(others, others, gain_sem.at[2]).wait()
    others = shares.at[pl.ds(0, FRAMES - 1), pl.ds(0, 1)]
    pltpu.make_async_copy(others, others, gain_sem.at[4]).wait()
    for a, dst in enumerate((dq_hbm, dk_hbm, dv_hbm)):
        pltpu.make_async_copy(outs.at[a], dst, out_sem.at[a]).wait()


def main_call(q, k, v, c, q_gain, k_gain, frames, heights, widths, count):
    size = q_gain.shape[0]
    any_spec = pl.BlockSpec(memory_space=pl.ANY)
    vmem = pl.BlockSpec(memory_space=pltpu.VMEM)
    smem = pl.BlockSpec(memory_space=pltpu.SMEM)
    grad = jax.ShapeDtypeStruct((SPOTS, CHANNELS), BF16)
    share = jax.ShapeDtypeStruct((1, size), F32)
    arrays = (q, k, v, c, q_gain.reshape(1, size), k_gain.reshape(1, size))
    arrays = [pltpu.with_memory_space_constraint(x, pltpu.HBM) for x in arrays]
    arrays += [frames, heights, widths]
    return pl.pallas_call(
        functools.partial(main_kernel, count, size),
        out_shape=(grad, grad, grad, share, share),
        in_specs=[any_spec] * 6 + [smem] * 3,
        out_specs=(any_spec, any_spec, any_spec, vmem, vmem),
        scratch_shapes=[
            pltpu.VMEM((4, SPOTS, CHANNELS), BF16),
            pltpu.VMEM((HEADS, 4, 256, DIM), BF16),
            pltpu.VMEM((HEADS, 3, 256, DIM), BF16),
            pltpu.VMEM((HEADS, 3, SPOTS, DIM), BF16),
            pltpu.VMEM((HEADS, 3, SPOTS, DIM), F32),
            pltpu.VMEM((3, SPOTS, CHANNELS), BF16),
            pltpu.VMEM((256, 256), F32),
            pltpu.VMEM((2 * HEADS, DIM), F32),
            pltpu.VMEM((2 * HEADS, DIM), F32),
            pltpu.VMEM((8, DIM), F32),
            pltpu.VMEM((8, DIM), F32),
            pltpu.VMEM((count, 8, DIM), F32),
            pltpu.VMEM((count, 8, DIM), F32),
            pltpu.VMEM((count, 8, DIM), F32),
            pltpu.VMEM((8, DIM), F32),
            pltpu.VMEM((FRAMES, 8, DIM), F32),
            pltpu.VMEM((2, 1, size), F32),
            pltpu.SemaphoreType.REGULAR((2,)),
            pltpu.SemaphoreType.DMA((2,)),
            pltpu.SemaphoreType.DMA((4,)),
            pltpu.SemaphoreType.DMA((HEADS,)),
            pltpu.SemaphoreType.DMA((HEADS,)),
            pltpu.SemaphoreType.DMA((HEADS,)),
            pltpu.SemaphoreType.DMA((HEADS,)),
            pltpu.SemaphoreType.DMA((HEADS,)),
            pltpu.SemaphoreType.DMA((3,)),
            pltpu.SemaphoreType.DMA((6,)),
        ],
        compiler_params=pltpu.CompilerParams(
            collective_id=1, has_side_effects=True, vmem_limit_bytes=40 << 20
        ),
        name="axial",
    )(*arrays)


def emit_kernel(*refs):
    half = len(refs) // 2
    sem = refs[-1]
    copies = [
        pltpu.make_async_copy(src, dst, sem.at[i])
        for i, (src, dst) in enumerate(zip(refs[:half], refs[half:-1]))
    ]
    for copy in copies:
        copy.start()
    for copy in copies:
        copy.wait()


def emit(arrays):
    any_spec = pl.BlockSpec(memory_space=pl.ANY)
    vmem = pl.BlockSpec(memory_space=pltpu.VMEM)
    return pl.pallas_call(
        emit_kernel,
        out_shape=tuple(jax.ShapeDtypeStruct(x.shape, x.dtype) for x in arrays),
        in_specs=[vmem] * len(arrays),
        out_specs=(any_spec,) * len(arrays),
        scratch_shapes=[pltpu.SemaphoreType.DMA((len(arrays),))],
        compiler_params=pltpu.CompilerParams(vmem_limit_bytes=8 << 20),
        name="emit",
    )(*arrays)


def shards(query_input, key_input, value_input, cotangent, q_gain, k_gain, frames, heights, widths):
    count = lax.axis_size("dp")
    flat = (SPOTS, CHANNELS)
    results = main_call(
        query_input.reshape(flat),
        key_input.reshape(flat),
        value_input.reshape(flat),
        cotangent.reshape(flat),
        q_gain,
        k_gain,
        frames,
        heights,
        widths,
        count,
    )
    query_grad, key_grad, value_grad, share_q, share_k = emit(results)
    full = (1, 1, SPOTS, CHANNELS)
    return (
        query_grad.reshape(full),
        key_grad.reshape(full),
        value_grad.reshape(full),
        share_q.reshape(-1),
        share_k.reshape(-1),
    )


def solution(mesh):
    tokens = P("dp", "seq", None, None)
    return jax.shard_map(
        shards,
        mesh=mesh,
        in_specs=(tokens,) * 4 + (P("dp"),) * 5,
        out_specs=(tokens,) * 3 + (P("dp"),) * 2,
        check_vma=False,
    )
```

```python
import functools
import math

import jax
import jax.numpy as jnp
from jax import lax
from jax.experimental import pallas as pl
from jax.experimental.pallas import tpu as pltpu
from jax.sharding import PartitionSpec as P

HEADS = 12
DIM = 128
COLS = 16
FRAMES = 16
SPOTS = 240
BLOCK = 16
CHANNELS = HEADS * DIM
AHEAD = 8
AHEAD2 = 4
EARLY = 8
PAIR_S = 2
PAIR_T = 2
FROM = 12
FIRST = 6
EPS = 1e-06
NEGATIVE = -1e30
FAR = -2e30
SCALE = 1.0 / math.sqrt(DIM)
LOG2E = math.log2(math.e)
MESH = pl.DeviceIdType.MESH
F32 = jnp.float32
BF16 = jnp.bfloat16


def dot(a, b, dims):
    return lax.dot_general(a, b, (dims, ((), ())), preferred_element_type=F32)


def inverse_norm(values):
    return lax.rsqrt(jnp.sum(values * values, axis=-1, keepdims=True) * (1.0 / DIM) + EPS)


def attend(queries, keys, values, cotan, bias):
    scores = dot(keys, queries, ((1,), (1,))) * (SCALE * LOG2E) + bias
    dprobs = dot(values, cotan, ((1,), (1,)))
    expo = jnp.exp2(scores - jnp.max(scores, axis=0, keepdims=True))
    probs = expo * (1.0 / jnp.sum(expo, axis=0, keepdims=True))
    value_part = dot(probs.astype(BF16), cotan, ((1,), (0,)))
    delta = jnp.sum(probs * dprobs, axis=0, keepdims=True)
    dscores = (probs * (dprobs - delta) * SCALE).astype(BF16)
    key_part = dot(dscores, queries, ((1,), (0,)))
    query_part = dot(dscores, keys, ((0,), (0,)))
    return query_part, key_part, value_part


def partner(me, i):
    return i - 1 + jnp.where(i > me, 1, 0)


def idle_of(head):
    return jnp.where(head < 11, head, 15)


def piece_of(i, size):
    start = i * size
    return start // DIM, start % DIM, start % DIM + size > DIM


def lead_of(place, count):
    return lax.rem(place + count // 2, count)


def main_kernel(
    count, size,
    q_hbm, k_hbm, v_hbm, c_hbm, q_gain, k_gain, frames, heights, widths,
    dq_hbm, dk_hbm, dv_hbm, share_q, share_k,
    stack, recv, tout, ret, sgrad, outs, bias_t, gains, gpart, piece, spare, pieces, cut, cuts, sums, shares,
    gain_rows, met_sem, small_sem, load_sem, fwd_send, fwd_recv, own_sem, back_send, back_recv, out_sem, gain_sem,
):
    me = lax.axis_index("seq")
    clip = lax.axis_index("dp")

    leads = clip == lead_of(me, count)

    loads = [
        pltpu.make_async_copy(src, stack.at[a], load_sem.at[a])
        for a, src in enumerate((q_hbm, k_hbm, v_hbm, c_hbm))
    ]
    smalls = [
        pltpu.make_async_copy(src, dst, small_sem.at[a])
        for a, (src, dst) in enumerate(
            ((q_gain, gain_rows.at[0]), (k_gain, gain_rows.at[1]))
        )
    ]
    barrier = pltpu.get_barrier_semaphore()

    def greet(i, carry):
        to = lax.rem(me + i, FRAMES)

        @pl.when(clip != lead_of(to, count))
        def _():
            pl.semaphore_signal(barrier, inc=1, device_id={"seq": to}, device_id_type=MESH)

        return carry

    lax.fori_loop(1, FRAMES, greet, 0)
    for load in loads:
        load.start()
    for small in smalls:
        small.start()

    @pl.when(jnp.logical_not(leads))
    def _():
        pl.semaphore_signal(
            barrier, inc=1, device_id={"dp": lead_of(me, count)}, device_id_type=MESH
        )

    for load in loads:
        load.wait()

    @pl.when(jnp.logical_not(leads))
    def _():
        pl.semaphore_wait(barrier, FRAMES - 1)

    mate = lax.rem(me + FRAMES - 1, FRAMES)

    @pl.when(clip == lead_of(mate, count))
    def _():
        pl.semaphore_signal(met_sem.at[0], inc=1, device_id={"seq": mate}, device_id_type=MESH)

    @pl.when(leads)
    def _():
        pl.semaphore_wait(met_sem.at[0], 1)

    def lanes(head):
        return pl.ds(pl.multiple_of(head * DIM, DIM), DIM)

    def rows(block):
        return pl.ds(pl.multiple_of(block * BLOCK, BLOCK), BLOCK)

    def send_unit(head, to):
        idle = idle_of(head)
        block = jnp.where(to < 15, to, head)

        @pl.when((to != idle) & (to != me))
        def _():
            pltpu.make_async_remote_copy(
                src_ref=stack.at[:, rows(block), lanes(head)],
                dst_ref=recv.at[head, :, rows(me), :],
                send_sem=fwd_send.at[head],
                recv_sem=fwd_recv.at[head],
                device_id={"seq": to},
                device_id_type=MESH,
            ).start()

        @pl.when((to != idle) & (to == me))
        def _():
            pltpu.make_async_copy(
                stack.at[:, rows(block), lanes(head)],
                recv.at[head, :, rows(me), :],
                own_sem.at[head],
            ).start()

    def send_head(head, carry):
        def one(i, inner):
            send_unit(head, lax.rem(i + FROM, FRAMES))
            return inner

        lax.fori_loop(0, FRAMES, one, 0)
        return carry

    ahead = jnp.where(clip < count // 2, AHEAD, AHEAD2)
    lax.fori_loop(0, ahead, send_head, 0)

    for small in smalls:
        small.wait()
    shift = lax.rem(clip * size, DIM)
    piece[...] = jnp.zeros_like(piece)
    spare[...] = jnp.zeros_like(spare)
    piece[0:1, 0:size] = gain_rows[0]
    spare[0:1, 0:size] = gain_rows[1]
    piece[...] = pltpu.roll(piece[...] + pltpu.roll(spare[...], DIM // 2, 1), shift, 1)
    pieces[clip, 0:1] = piece[0:1]

    @pl.when(leads)
    def _():
        pl.semaphore_wait(barrier, count - 1)

        def tell(i, carry):
            to = lax.rem(clip + i, count)
            pl.semaphore_signal(met_sem.at[1], inc=1, device_id={"dp": to}, device_id_type=MESH)
            return carry

        lax.fori_loop(1, count, tell, 0)

    @pl.when(jnp.logical_not(leads))
    def _():
        pl.semaphore_wait(met_sem.at[1], 1)

    def send_piece(i, carry):
        pltpu.make_async_remote_copy(
            src_ref=piece.at[pl.ds(0, 1)],
            dst_ref=pieces.at[clip, pl.ds(0, 1)],
            send_sem=gain_sem.at[0],
            recv_sem=gain_sem.at[1],
            device_id={"dp": lax.rem(clip + i, count)},
            device_id_type=MESH,
        ).start()
        return carry

    lax.fori_loop(1, count, send_piece, 0)
    lax.fori_loop(ahead, HEADS, send_head, 0)

    others = pieces.at[pl.ds(0, count - 1), pl.ds(0, 1)]
    pltpu.make_async_copy(others, others, gain_sem.at[1]).wait()
    lane = lax.broadcasted_iota(jnp.int32, (1, DIM), 1)
    total = [jnp.zeros((1, DIM), F32) for _ in range(2 * HEADS)]
    for i in range(count):
        at, off, spills = piece_of(i, size)
        row = pieces[i, 0:1]
        for a in range(2):
            if a:
                row = pltpu.roll(row, DIM // 2, 1)
            total[at + a * HEADS] += jnp.where((lane >= off) & (lane < off + size), row, 0.0)
            if spills:
                total[at + 1 + a * HEADS] += jnp.where(lane < off + size - DIM, row, 0.0)
    for at in range(2 * HEADS):
        gains[at : at + 1, :] = total[at]

    count_f, count_h, count_w = frames[0], heights[0], widths[0]

    def spot_fits(spot):
        return (spot // COLS < count_h) & (spot % COLS < count_w)

    spot = lax.broadcasted_iota(jnp.int32, (SPOTS, 1), 0)
    valid_s = spot_fits(spot) & (me < count_f)
    bias_s = jnp.where(valid_s, 0.0, NEGATIVE).astype(F32)
    cot_s = jnp.where(valid_s, 1.0, 0.0).astype(BF16)

    def spatial_head(head):
        q32 = stack[0, :, lanes(head)].astype(F32)
        k32 = stack[1, :, lanes(head)].astype(F32)
        gain_q, gain_k = gains[pl.ds(head, 1), :], gains[pl.ds(head + HEADS, 1), :]
        scaled_q, scaled_k = q32 * inverse_norm(q32), k32 * inverse_norm(k32)
        normed_q = (scaled_q * gain_q).astype(BF16)
        normed_k = (scaled_k * gain_k).astype(BF16)
        cotan = stack[3, :, lanes(head)] * cot_s
        part_q, part_k, part_v = attend(normed_q, normed_k, stack[2, :, lanes(head)], cotan, bias_s)
        sgrad[head, 0] = part_q
        sgrad[head, 1] = part_k
        sgrad[head, 2] = part_v
        gpart[pl.ds(head, 1), :] = jnp.sum(part_q * scaled_q, axis=0, keepdims=True)
        gpart[pl.ds(head + HEADS, 1), :] = jnp.sum(part_k * scaled_k, axis=0, keepdims=True)

    def spatial(step, carry):
        for j in range(PAIR_S):
            spatial_head(step * PAIR_S + j)
        return carry

    lax.fori_loop(0, HEADS // PAIR_S, spatial, 0)

    line = lax.broadcasted_iota(jnp.int32, (256, 1), 0)
    key_at = lax.broadcasted_iota(jnp.int32, (256, 256), 0)
    query_at = lax.broadcasted_iota(jnp.int32, (256, 256), 1)
    bias_t[...] = jnp.where(key_at % BLOCK == query_at % BLOCK, 0.0, FAR).astype(F32)

    units = jnp.where((me >= 11) & (me < 15), 12, 11)

    def head_of(unit):
        return unit + jnp.where((me < 11) & (unit >= me), 1, 0)

    def send_back(unit, carry):
        head = head_of(unit)
        block = jnp.where(me < 15, me, head)

        def send_one(i, inner):
            to = partner(me, i)
            pltpu.make_async_remote_copy(
                src_ref=tout.at[head, :, rows(to), :],
                dst_ref=ret.at[head, :, rows(block), :],
                send_sem=back_send.at[head],
                recv_sem=back_recv.at[head],
                device_id={"seq": to},
                device_id_type=MESH,
            ).start()
            return inner

        lax.fori_loop(1, 16, send_one, 0)
        pltpu.make_async_copy(
            tout.at[head, :, rows(me), :], ret.at[head, :, rows(block), :], own_sem.at[head]
        ).start()
        return carry

    def arrive(head):
        whole, own = recv.at[head, :, pl.ds(0, 240), :], recv.at[head, :, pl.ds(0, 16), :]
        pltpu.make_async_copy(whole, whole, fwd_recv.at[head]).wait()
        pltpu.make_async_copy(own, own, own_sem.at[head]).wait()

    def temporal_head(head):
        block = jnp.where(me < 15, me, head)
        valid_t = spot_fits(block * BLOCK + line % BLOCK) & (line // BLOCK < count_f)
        bias = bias_t[...] + jnp.where(valid_t, 0.0, NEGATIVE).astype(F32)
        q32 = recv[head, 0].astype(F32)
        k32 = recv[head, 1].astype(F32)
        gain_q, gain_k = gains[pl.ds(head, 1), :], gains[pl.ds(head + HEADS, 1), :]
        scaled_q, scaled_k = q32 * inverse_norm(q32), k32 * inverse_norm(k32)
        normed_q = (scaled_q * gain_q).astype(BF16)
        normed_k = (scaled_k * gain_k).astype(BF16)
        cotan = recv[head, 3] * jnp.where(valid_t, 1.0, 0.0).astype(BF16)
        part_q, part_k, part_v = attend(normed_q, normed_k, recv[head, 2], cotan, bias)
        part_q, part_k = part_q.astype(BF16), part_k.astype(BF16)
        tout[head, 0] = part_q
        tout[head, 1] = part_k
        tout[head, 2] = part_v.astype(BF16)
        gpart[pl.ds(head, 1), :] += jnp.sum(part_q.astype(F32) * scaled_q, axis=0, keepdims=True)
        gpart[pl.ds(head + HEADS, 1), :] += jnp.sum(
            part_k.astype(F32) * scaled_k, axis=0, keepdims=True
        )

    def temporal(step, carry):
        heads = [head_of(step * PAIR_T + j) for j in range(PAIR_T)]
        for head in heads:
            arrive(head)
        for head in heads:
            temporal_head(head)
        return carry

    def temporal_and_back(unit, carry):
        arrive(head_of(unit))
        temporal_head(head_of(unit))
        return send_back(unit, carry)

    lax.fori_loop(0, EARLY, temporal_and_back, 0)
    lax.fori_loop(EARLY // PAIR_T, 10 // PAIR_T, temporal, 0)
    arrive(head_of(10))
    temporal_head(head_of(10))

    @pl.when((me >= 11) & (me < 15))
    def _():
        arrive(11)
        temporal_head(11)

    for i in range(count):
        at, off, spills = piece_of(i, size)
        parts = []
        for a in range(2):
            row = gpart[at + a * HEADS : at + a * HEADS + 1, :]
            if spills:
                row = jnp.where(lane >= off, row, gpart[at + a * HEADS + 1 : at + a * HEADS + 2, :])
            parts.append(row)
        inside = (lane >= off) & (lane < off + size) | (lane < off + size - DIM)
        cut[i, 0:1, :] = jnp.where(inside, parts[0], pltpu.roll(parts[1], DIM // 2, 1))
    cuts[clip, 0:1] = cut[clip, 0:1]

    def send_cut(i, carry):
        to = lax.rem(clip + i, count)
        pltpu.make_async_remote_copy(
            src_ref=cut.at[to, pl.ds(0, 1)],
            dst_ref=cuts.at[clip, pl.ds(0, 1)],
            send_sem=gain_sem.at[2],
            recv_sem=gain_sem.at[3],
            device_id={"dp": to},
            device_id_type=MESH,
        ).start()
        return carry

    lax.fori_loop(1, count, send_cut, 0)
    lax.fori_loop(EARLY, units, send_back, 0)

    def finish(head, carry):
        idle = idle_of(head)

        @pl.when(me != idle)
        def _():
            pltpu.make_async_copy(
                ret.at[head, :, pl.ds(0, 224), :], ret.at[head, :, pl.ds(0, 224), :], back_recv.at[head]
            ).wait()
            pltpu.make_async_copy(
                ret.at[head, :, pl.ds(0, 16), :], ret.at[head, :, pl.ds(0, 16), :], own_sem.at[head]
            ).wait()

        @pl.when(me == idle)
        def _():
            pltpu.make_async_copy(ret.at[head], ret.at[head], back_recv.at[head]).wait()

        for a in range(2):
            raw = stack[a, :, lanes(head)].astype(F32)
            inverse = inverse_norm(raw)
            gain = gains[pl.ds(head + HEADS * a, 1), :]
            scaled = gain * (sgrad[head, a] + ret[head, a].astype(F32))
            mean = jnp.sum(scaled * raw, axis=-1, keepdims=True) * (1.0 / DIM)
            outs[a, :, lanes(head)] = (
                inverse * scaled - raw * (inverse * inverse * inverse) * mean
            ).astype(BF16)
        outs[2, :, lanes(head)] = (sgrad[head, 2] + ret[head, 2].astype(F32)).astype(BF16)
        for a, dst in enumerate((dq_hbm, dk_hbm, dv_hbm)):
            pltpu.make_async_copy(
                outs.at[a, :, lanes(head)], dst.at[:, lanes(head)], out_sem.at[a]
            ).start()
        return carry

    lax.fori_loop(0, FIRST, finish, 0)

    others = cuts.at[pl.ds(0, count - 1), pl.ds(0, 1)]
    pltpu.make_async_copy(others, others, gain_sem.at[3]).wait()
    summed = jnp.broadcast_to(jnp.sum(cuts[:, 0:1], axis=0), (8, DIM))
    sums[...] = pltpu.roll(summed, lax.rem(DIM - shift, DIM), 1)
    shares[me, 0:1] = sums[0:1]

    def send_sums(i, carry):
        pltpu.make_async_remote_copy(
            src_ref=sums.at[pl.ds(0, 1)],
            dst_ref=shares.at[me, pl.ds(0, 1)],
            send_sem=gain_sem.at[4],
            recv_sem=gain_sem.at[5],
            device_id={"seq": lax.rem(me + i, FRAMES)},
            device_id_type=MESH,
        ).start()
        return carry

    lax.fori_loop(1, FRAMES, send_sums, 0)

    lax.fori_loop(FIRST, HEADS, finish, 0)

    others = shares.at[pl.ds(0, FRAMES - 1), pl.ds(0, 1)]
    pltpu.make_async_copy(others, others, gain_sem.at[5]).wait()
    summed = jnp.sum(shares[:, 0:1], axis=0)
    share_q[...] = summed[:, 0:size]
    share_k[...] = pltpu.roll(summed, DIM // 2, 1)[:, 0:size]

    def drain(head, carry):
        idle = idle_of(head)

        @pl.when(me != idle)
        def _():
            pltpu.make_async_copy(
                recv.at[head, :, pl.ds(0, 224), :], recv.at[head, :, pl.ds(0, 224), :], fwd_send.at[head]
            ).wait()
            pltpu.make_async_copy(
                tout.at[head, :, pl.ds(0, 240), :], tout.at[head, :, pl.ds(0, 240), :], back_send.at[head]
            ).wait()

        @pl.when(me == idle)
        def _():
            pltpu.make_async_copy(
                recv.at[head, :, pl.ds(0, 240), :], recv.at[head, :, pl.ds(0, 240), :], fwd_send.at[head]
            ).wait()

        return carry

    lax.fori_loop(0, HEADS, drain, 0)
    others = cuts.at[pl.ds(0, count - 1), pl.ds(0, 1)]
    pltpu.make_async_copy(others, others, gain_sem.at[0]).wait()
    pltpu.make_async_copy(others, others, gain_sem.at[2]).wait()
    others = shares.at[pl.ds(0, FRAMES - 1), pl.ds(0, 1)]
    pltpu.make_async_copy(others, others, gain_sem.at[4]).wait()
    for a, dst in enumerate((dq_hbm, dk_hbm, dv_hbm)):
        pltpu.make_async_copy(outs.at[a], dst, out_sem.at[a]).wait()


def main_call(q, k, v, c, q_gain, k_gain, frames, heights, widths, count):
    size = q_gain.shape[0]
    any_spec = pl.BlockSpec(memory_space=pl.ANY)
    vmem = pl.BlockSpec(memory_space=pltpu.VMEM)
    smem = pl.BlockSpec(memory_space=pltpu.SMEM)
    grad = jax.ShapeDtypeStruct((SPOTS, CHANNELS), BF16)
    share = jax.ShapeDtypeStruct((1, size), F32)
    arrays = (q, k, v, c, q_gain.reshape(1, size), k_gain.reshape(1, size))
    arrays = [pltpu.with_memory_space_constraint(x, pltpu.HBM) for x in arrays]
    arrays += [frames, heights, widths]
    return pl.pallas_call(
        functools.partial(main_kernel, count, size),
        out_shape=(grad, grad, grad, share, share),
        in_specs=[any_spec] * 6 + [smem] * 3,
        out_specs=(any_spec, any_spec, any_spec, vmem, vmem),
        scratch_shapes=[
            pltpu.VMEM((4, SPOTS, CHANNELS), BF16),
            pltpu.VMEM((HEADS, 4, 256, DIM), BF16),
            pltpu.VMEM((HEADS, 3, 256, DIM), BF16),
            pltpu.VMEM((HEADS, 3, SPOTS, DIM), BF16),
            pltpu.VMEM((HEADS, 3, SPOTS, DIM), F32),
            pltpu.VMEM((3, SPOTS, CHANNELS), BF16),
            pltpu.VMEM((256, 256), F32),
            pltpu.VMEM((2 * HEADS, DIM), F32),
            pltpu.VMEM((2 * HEADS, DIM), F32),
            pltpu.VMEM((8, DIM), F32),
            pltpu.VMEM((8, DIM), F32),
            pltpu.VMEM((count, 8, DIM), F32),
            pltpu.VMEM((count, 8, DIM), F32),
            pltpu.VMEM((count, 8, DIM), F32),
            pltpu.VMEM((8, DIM), F32),
            pltpu.VMEM((FRAMES, 8, DIM), F32),
            pltpu.VMEM((2, 1, size), F32),
            pltpu.SemaphoreType.REGULAR((2,)),
            pltpu.SemaphoreType.DMA((2,)),
            pltpu.SemaphoreType.DMA((4,)),
            pltpu.SemaphoreType.DMA((HEADS,)),
            pltpu.SemaphoreType.DMA((HEADS,)),
            pltpu.SemaphoreType.DMA((HEADS,)),
            pltpu.SemaphoreType.DMA((HEADS,)),
            pltpu.SemaphoreType.DMA((HEADS,)),
            pltpu.SemaphoreType.DMA((3,)),
            pltpu.SemaphoreType.DMA((6,)),
        ],
        compiler_params=pltpu.CompilerParams(
            collective_id=1, has_side_effects=True, vmem_limit_bytes=40 << 20
        ),
        name="axial",
    )(*arrays)


def emit_kernel(*refs):
    half = len(refs) // 2
    sem = refs[-1]
    copies = [
        pltpu.make_async_copy(src, dst, sem.at[i])
        for i, (src, dst) in enumerate(zip(refs[:half], refs[half:-1]))
    ]
    for copy in copies:
        copy.start()
    for copy in copies:
        copy.wait()


def emit(arrays):
    any_spec = pl.BlockSpec(memory_space=pl.ANY)
    vmem = pl.BlockSpec(memory_space=pltpu.VMEM)
    return pl.pallas_call(
        emit_kernel,
        out_shape=tuple(jax.ShapeDtypeStruct(x.shape, x.dtype) for x in arrays),
        in_specs=[vmem] * len(arrays),
        out_specs=(any_spec,) * len(arrays),
        scratch_shapes=[pltpu.SemaphoreType.DMA((len(arrays),))],
        compiler_params=pltpu.CompilerParams(vmem_limit_bytes=8 << 20),
        name="emit",
    )(*arrays)


def shards(query_input, key_input, value_input, cotangent, q_gain, k_gain, frames, heights, widths):
    count = lax.axis_size("dp")
    flat = (SPOTS, CHANNELS)
    results = main_call(
        query_input.reshape(flat),
        key_input.reshape(flat),
        value_input.reshape(flat),
        cotangent.reshape(flat),
        q_gain,
        k_gain,
        frames,
        heights,
        widths,
        count,
    )
    query_grad, key_grad, value_grad, share_q, share_k = emit(results)
    full = (1, 1, SPOTS, CHANNELS)
    return (
        query_grad.reshape(full),
        key_grad.reshape(full),
        value_grad.reshape(full),
        share_q.reshape(-1),
        share_k.reshape(-1),
    )


def solution(mesh):
    tokens = P("dp", "seq", None, None)
    return jax.shard_map(
        shards,
        mesh=mesh,
        in_specs=(tokens,) * 4 + (P("dp"),) * 5,
        out_specs=(tokens,) * 3 + (P("dp"),) * 2,
        check_vma=False,
    )
```

```python
import functools
import math

import jax
import jax.numpy as jnp
from jax import lax
from jax.experimental import pallas as pl
from jax.experimental.pallas import tpu as pltpu
from jax.sharding import PartitionSpec as P

HEADS = 12
DIM = 128
COLS = 16
FRAMES = 16
SPOTS = 240
BLOCK = 16
CHANNELS = HEADS * DIM
AHEAD = 10
AHEAD2 = 5
EARLY = 8
PAIR_S = 3
PAIR_T = 2
FROM = 12
FIRST = 6
EPS = 1e-06
NEGATIVE = -1e30
FAR = -2e30
SCALE = 1.0 / math.sqrt(DIM)
LOG2E = math.log2(math.e)
MESH = pl.DeviceIdType.MESH
F32 = jnp.float32
BF16 = jnp.bfloat16


def dot(a, b, dims):
    return lax.dot_general(a, b, (dims, ((), ())), preferred_element_type=F32)


def inverse_norm(values):
    return lax.rsqrt(jnp.sum(values * values, axis=-1, keepdims=True) * (1.0 / DIM) + EPS)


def attend(queries, keys, values, cotan, bias):
    scores = dot(keys, queries, ((1,), (1,))) * (SCALE * LOG2E) + bias
    dprobs = dot(values, cotan, ((1,), (1,)))
    expo = jnp.exp2(scores - jnp.max(scores, axis=0, keepdims=True))
    probs = expo * (1.0 / jnp.sum(expo, axis=0, keepdims=True))
    value_part = dot(probs.astype(BF16), cotan, ((1,), (0,)))
    delta = jnp.sum(probs * dprobs, axis=0, keepdims=True)
    dscores = (probs * (dprobs - delta) * SCALE).astype(BF16)
    key_part = dot(dscores, queries, ((1,), (0,)))
    query_part = dot(dscores, keys, ((0,), (0,)))
    return query_part, key_part, value_part


def partner(me, i):
    return i - 1 + jnp.where(i > me, 1, 0)


def idle_of(head):
    return jnp.where(head < 11, head, 15)


def piece_of(i, size):
    start = i * size
    return start // DIM, start % DIM, start % DIM + size > DIM


def lead_of(place, count):
    return lax.rem(place + count // 2, count)


def main_kernel(
    count, size,
    q_hbm, k_hbm, v_hbm, c_hbm, q_gain, k_gain, frames, heights, widths,
    dq_hbm, dk_hbm, dv_hbm, share_q, share_k,
    stack, recv, tout, ret, sgrad, outs, bias_t, gains, gpart, piece, spare, pieces, cut, cuts, sums, shares,
    gain_rows, met_sem, small_sem, load_sem, fwd_send, fwd_recv, own_sem, back_send, back_recv, out_sem, gain_sem,
):
    me = lax.axis_index("seq")
    clip = lax.axis_index("dp")

    leads = clip == lead_of(me, count)

    loads = [
        pltpu.make_async_copy(src, stack.at[a], load_sem.at[a])
        for a, src in enumerate((q_hbm, k_hbm, v_hbm, c_hbm))
    ]
    smalls = [
        pltpu.make_async_copy(src, dst, small_sem.at[a])
        for a, (src, dst) in enumerate(
            ((q_gain, gain_rows.at[0]), (k_gain, gain_rows.at[1]))
        )
    ]
    barrier = pltpu.get_barrier_semaphore()

    def greet(i, carry):
        to = lax.rem(me + i, FRAMES)

        @pl.when(clip != lead_of(to, count))
        def _():
            pl.semaphore_signal(barrier, inc=1, device_id={"seq": to}, device_id_type=MESH)

        return carry

    lax.fori_loop(1, FRAMES, greet, 0)
    for load in loads:
        load.start()
    for small in smalls:
        small.start()

    @pl.when(jnp.logical_not(leads))
    def _():
        pl.semaphore_signal(
            barrier, inc=1, device_id={"dp": lead_of(me, count)}, device_id_type=MESH
        )

    for load in loads:
        load.wait()

    @pl.when(jnp.logical_not(leads))
    def _():
        pl.semaphore_wait(barrier, FRAMES - 1)

    mate = lax.rem(me + FRAMES - 1, FRAMES)

    @pl.when(clip == lead_of(mate, count))
    def _():
        pl.semaphore_signal(met_sem.at[0], inc=1, device_id={"seq": mate}, device_id_type=MESH)

    @pl.when(leads)
    def _():
        pl.semaphore_wait(met_sem.at[0], 1)

    def lanes(head):
        return pl.ds(pl.multiple_of(head * DIM, DIM), DIM)

    def rows(block):
        return pl.ds(pl.multiple_of(block * BLOCK, BLOCK), BLOCK)

    def send_unit(head, to):
        idle = idle_of(head)
        block = jnp.where(to < 15, to, head)

        @pl.when((to != idle) & (to != me))
        def _():
            pltpu.make_async_remote_copy(
                src_ref=stack.at[:, rows(block), lanes(head)],
                dst_ref=recv.at[head, :, rows(me), :],
                send_sem=fwd_send.at[head],
                recv_sem=fwd_recv.at[head],
                device_id={"seq": to},
                device_id_type=MESH,
            ).start()

        @pl.when((to != idle) & (to == me))
        def _():
            pltpu.make_async_copy(
                stack.at[:, rows(block), lanes(head)],
                recv.at[head, :, rows(me), :],
                own_sem.at[head],
            ).start()

    def send_head(head, carry):
        def one(i, inner):
            send_unit(head, lax.rem(i + FROM, FRAMES))
            return inner

        lax.fori_loop(0, FRAMES, one, 0)
        return carry

    ahead = jnp.where(clip < count // 2, AHEAD, AHEAD2)
    lax.fori_loop(0, ahead, send_head, 0)

    for small in smalls:
        small.wait()
    shift = lax.rem(clip * size, DIM)
    piece[...] = jnp.zeros_like(piece)
    spare[...] = jnp.zeros_like(spare)
    piece[0:1, 0:size] = gain_rows[0]
    spare[0:1, 0:size] = gain_rows[1]
    piece[...] = pltpu.roll(piece[...] + pltpu.roll(spare[...], DIM // 2, 1), shift, 1)
    pieces[clip, 0:1] = piece[0:1]

    @pl.when(leads)
    def _():
        pl.semaphore_wait(barrier, count - 1)

        def tell(i, carry):
            to = lax.rem(clip + i, count)
            pl.semaphore_signal(met_sem.at[1], inc=1, device_id={"dp": to}, device_id_type=MESH)
            return carry

        lax.fori_loop(1, count, tell, 0)

    @pl.when(jnp.logical_not(leads))
    def _():
        pl.semaphore_wait(met_sem.at[1], 1)

    def send_piece(i, carry):
        pltpu.make_async_remote_copy(
            src_ref=piece.at[pl.ds(0, 1)],
            dst_ref=pieces.at[clip, pl.ds(0, 1)],
            send_sem=gain_sem.at[0],
            recv_sem=gain_sem.at[1],
            device_id={"dp": lax.rem(clip + i, count)},
            device_id_type=MESH,
        ).start()
        return carry

    lax.fori_loop(1, count, send_piece, 0)
    lax.fori_loop(ahead, HEADS, send_head, 0)

    others = pieces.at[pl.ds(0, count - 1), pl.ds(0, 1)]
    pltpu.make_async_copy(others, others, gain_sem.at[1]).wait()
    lane = lax.broadcasted_iota(jnp.int32, (1, DIM), 1)
    total = [jnp.zeros((1, DIM), F32) for _ in range(2 * HEADS)]
    for i in range(count):
        at, off, spills = piece_of(i, size)
        row = pieces[i, 0:1]
        for a in range(2):
            if a:
                row = pltpu.roll(row, DIM // 2, 1)
            total[at + a * HEADS] += jnp.where((lane >= off) & (lane < off + size), row, 0.0)
            if spills:
                total[at + 1 + a * HEADS] += jnp.where(lane < off + size - DIM, row, 0.0)
    for at in range(2 * HEADS):
        gains[at : at + 1, :] = total[at]

    count_f, count_h, count_w = frames[0], heights[0], widths[0]

    def spot_fits(spot):
        return (spot // COLS < count_h) & (spot % COLS < count_w)

    spot = lax.broadcasted_iota(jnp.int32, (SPOTS, 1), 0)
    valid_s = spot_fits(spot) & (me < count_f)
    bias_s = jnp.where(valid_s, 0.0, NEGATIVE).astype(F32)
    cot_s = jnp.where(valid_s, 1.0, 0.0).astype(BF16)

    def spatial_head(head):
        q32 = stack[0, :, lanes(head)].astype(F32)
        k32 = stack[1, :, lanes(head)].astype(F32)
        gain_q, gain_k = gains[pl.ds(head, 1), :], gains[pl.ds(head + HEADS, 1), :]
        scaled_q, scaled_k = q32 * inverse_norm(q32), k32 * inverse_norm(k32)
        normed_q = (scaled_q * gain_q).astype(BF16)
        normed_k = (scaled_k * gain_k).astype(BF16)
        cotan = stack[3, :, lanes(head)] * cot_s
        part_q, part_k, part_v = attend(normed_q, normed_k, stack[2, :, lanes(head)], cotan, bias_s)
        sgrad[head, 0] = part_q
        sgrad[head, 1] = part_k
        sgrad[head, 2] = part_v
        gpart[pl.ds(head, 1), :] = jnp.sum(part_q * scaled_q, axis=0, keepdims=True)
        gpart[pl.ds(head + HEADS, 1), :] = jnp.sum(part_k * scaled_k, axis=0, keepdims=True)

    def spatial(step, carry):
        for j in range(PAIR_S):
            spatial_head(step * PAIR_S + j)
        return carry

    lax.fori_loop(0, HEADS // PAIR_S, spatial, 0)

    line = lax.broadcasted_iota(jnp.int32, (256, 1), 0)
    key_at = lax.broadcasted_iota(jnp.int32, (256, 256), 0)
    query_at = lax.broadcasted_iota(jnp.int32, (256, 256), 1)
    bias_t[...] = jnp.where(key_at % BLOCK == query_at % BLOCK, 0.0, FAR).astype(F32)

    units = jnp.where((me >= 11) & (me < 15), 12, 11)

    def head_of(unit):
        return unit + jnp.where((me < 11) & (unit >= me), 1, 0)

    def send_back(unit, carry):
        head = head_of(unit)
        block = jnp.where(me < 15, me, head)

        def send_one(i, inner):
            to = partner(me, i)
            pltpu.make_async_remote_copy(
                src_ref=tout.at[head, :, rows(to), :],
                dst_ref=ret.at[head, :, rows(block), :],
                send_sem=back_send.at[head],
                recv_sem=back_recv.at[head],
                device_id={"seq": to},
                device_id_type=MESH,
            ).start()
            return inner

        lax.fori_loop(1, 16, send_one, 0)
        pltpu.make_async_copy(
            tout.at[head, :, rows(me), :], ret.at[head, :, rows(block), :], own_sem.at[head]
        ).start()
        return carry

    def arrive(head):
        whole, own = recv.at[head, :, pl.ds(0, 240), :], recv.at[head, :, pl.ds(0, 16), :]
        pltpu.make_async_copy(whole, whole, fwd_recv.at[head]).wait()
        pltpu.make_async_copy(own, own, own_sem.at[head]).wait()

    def temporal_head(head):
        block = jnp.where(me < 15, me, head)
        valid_t = spot_fits(block * BLOCK + line % BLOCK) & (line // BLOCK < count_f)
        bias = bias_t[...] + jnp.where(valid_t, 0.0, NEGATIVE).astype(F32)
        q32 = recv[head, 0].astype(F32)
        k32 = recv[head, 1].astype(F32)
        gain_q, gain_k = gains[pl.ds(head, 1), :], gains[pl.ds(head + HEADS, 1), :]
        scaled_q, scaled_k = q32 * inverse_norm(q32), k32 * inverse_norm(k32)
        normed_q = (scaled_q * gain_q).astype(BF16)
        normed_k = (scaled_k * gain_k).astype(BF16)
        cotan = recv[head, 3] * jnp.where(valid_t, 1.0, 0.0).astype(BF16)
        part_q, part_k, part_v = attend(normed_q, normed_k, recv[head, 2], cotan, bias)
        part_q, part_k = part_q.astype(BF16), part_k.astype(BF16)
        tout[head, 0] = part_q
        tout[head, 1] = part_k
        tout[head, 2] = part_v.astype(BF16)
        gpart[pl.ds(head, 1), :] += jnp.sum(part_q.astype(F32) * scaled_q, axis=0, keepdims=True)
        gpart[pl.ds(head + HEADS, 1), :] += jnp.sum(
            part_k.astype(F32) * scaled_k, axis=0, keepdims=True
        )

    def temporal(step, carry):
        heads = [head_of(step * PAIR_T + j) for j in range(PAIR_T)]
        for head in heads:
            arrive(head)
        for head in heads:
            temporal_head(head)
        return carry

    def temporal_and_back(unit, carry):
        arrive(head_of(unit))
        temporal_head(head_of(unit))
        return send_back(unit, carry)

    lax.fori_loop(0, EARLY, temporal_and_back, 0)
    lax.fori_loop(EARLY // PAIR_T, 10 // PAIR_T, temporal, 0)
    arrive(head_of(10))
    temporal_head(head_of(10))

    @pl.when((me >= 11) & (me < 15))
    def _():
        arrive(11)
        temporal_head(11)

    for i in range(count):
        at, off, spills = piece_of(i, size)
        parts = []
        for a in range(2):
            row = gpart[at + a * HEADS : at + a * HEADS + 1, :]
            if spills:
                row = jnp.where(lane >= off, row, gpart[at + a * HEADS + 1 : at + a * HEADS + 2, :])
            parts.append(row)
        inside = (lane >= off) & (lane < off + size) | (lane < off + size - DIM)
        cut[i, 0:1, :] = jnp.where(inside, parts[0], pltpu.roll(parts[1], DIM // 2, 1))
    cuts[clip, 0:1] = cut[clip, 0:1]

    def send_cut(i, carry):
        to = lax.rem(clip + i, count)
        pltpu.make_async_remote_copy(
            src_ref=cut.at[to, pl.ds(0, 1)],
            dst_ref=cuts.at[clip, pl.ds(0, 1)],
            send_sem=gain_sem.at[2],
            recv_sem=gain_sem.at[3],
            device_id={"dp": to},
            device_id_type=MESH,
        ).start()
        return carry

    lax.fori_loop(1, count, send_cut, 0)
    lax.fori_loop(EARLY, units, send_back, 0)

    def finish(head, carry):
        idle = idle_of(head)

        @pl.when(me != idle)
        def _():
            pltpu.make_async_copy(
                ret.at[head, :, pl.ds(0, 224), :], ret.at[head, :, pl.ds(0, 224), :], back_recv.at[head]
            ).wait()
            pltpu.make_async_copy(
                ret.at[head, :, pl.ds(0, 16), :], ret.at[head, :, pl.ds(0, 16), :], own_sem.at[head]
            ).wait()

        @pl.when(me == idle)
        def _():
            pltpu.make_async_copy(ret.at[head], ret.at[head], back_recv.at[head]).wait()

        for a in range(2):
            raw = stack[a, :, lanes(head)].astype(F32)
            inverse = inverse_norm(raw)
            gain = gains[pl.ds(head + HEADS * a, 1), :]
            scaled = gain * (sgrad[head, a] + ret[head, a].astype(F32))
            mean = jnp.sum(scaled * raw, axis=-1, keepdims=True) * (1.0 / DIM)
            outs[a, :, lanes(head)] = (
                inverse * scaled - raw * (inverse * inverse * inverse) * mean
            ).astype(BF16)
        outs[2, :, lanes(head)] = (sgrad[head, 2] + ret[head, 2].astype(F32)).astype(BF16)
        for a, dst in enumerate((dq_hbm, dk_hbm, dv_hbm)):
            pltpu.make_async_copy(
                outs.at[a, :, lanes(head)], dst.at[:, lanes(head)], out_sem.at[a]
            ).start()
        return carry

    lax.fori_loop(0, FIRST, finish, 0)

    others = cuts.at[pl.ds(0, count - 1), pl.ds(0, 1)]
    pltpu.make_async_copy(others, others, gain_sem.at[3]).wait()
    summed = jnp.broadcast_to(jnp.sum(cuts[:, 0:1], axis=0), (8, DIM))
    sums[...] = pltpu.roll(summed, lax.rem(DIM - shift, DIM), 1)
    shares[me, 0:1] = sums[0:1]

    def send_sums(i, carry):
        pltpu.make_async_remote_copy(
            src_ref=sums.at[pl.ds(0, 1)],
            dst_ref=shares.at[me, pl.ds(0, 1)],
            send_sem=gain_sem.at[4],
            recv_sem=gain_sem.at[5],
            device_id={"seq": lax.rem(me + i, FRAMES)},
            device_id_type=MESH,
        ).start()
        return carry

    lax.fori_loop(1, FRAMES, send_sums, 0)

    lax.fori_loop(FIRST, HEADS, finish, 0)

    others = shares.at[pl.ds(0, FRAMES - 1), pl.ds(0, 1)]
    pltpu.make_async_copy(others, others, gain_sem.at[5]).wait()
    summed = jnp.sum(shares[:, 0:1], axis=0)
    share_q[...] = summed[:, 0:size]
    share_k[...] = pltpu.roll(summed, DIM // 2, 1)[:, 0:size]

    def drain(head, carry):
        idle = idle_of(head)

        @pl.when(me != idle)
        def _():
            pltpu.make_async_copy(
                recv.at[head, :, pl.ds(0, 224), :], recv.at[head, :, pl.ds(0, 224), :], fwd_send.at[head]
            ).wait()
            pltpu.make_async_copy(
                tout.at[head, :, pl.ds(0, 240), :], tout.at[head, :, pl.ds(0, 240), :], back_send.at[head]
            ).wait()

        @pl.when(me == idle)
        def _():
            pltpu.make_async_copy(
                recv.at[head, :, pl.ds(0, 240), :], recv.at[head, :, pl.ds(0, 240), :], fwd_send.at[head]
            ).wait()

        return carry

    lax.fori_loop(0, HEADS, drain, 0)
    others = cuts.at[pl.ds(0, count - 1), pl.ds(0, 1)]
    pltpu.make_async_copy(others, others, gain_sem.at[0]).wait()
    pltpu.make_async_copy(others, others, gain_sem.at[2]).wait()
    others = shares.at[pl.ds(0, FRAMES - 1), pl.ds(0, 1)]
    pltpu.make_async_copy(others, others, gain_sem.at[4]).wait()
    for a, dst in enumerate((dq_hbm, dk_hbm, dv_hbm)):
        pltpu.make_async_copy(outs.at[a], dst, out_sem.at[a]).wait()


def main_call(q, k, v, c, q_gain, k_gain, frames, heights, widths, count):
    size = q_gain.shape[0]
    any_spec = pl.BlockSpec(memory_space=pl.ANY)
    vmem = pl.BlockSpec(memory_space=pltpu.VMEM)
    smem = pl.BlockSpec(memory_space=pltpu.SMEM)
    grad = jax.ShapeDtypeStruct((SPOTS, CHANNELS), BF16)
    share = jax.ShapeDtypeStruct((1, size), F32)
    arrays = (q, k, v, c, q_gain.reshape(1, size), k_gain.reshape(1, size))
    arrays = [pltpu.with_memory_space_constraint(x, pltpu.HBM) for x in arrays]
    arrays += [frames, heights, widths]
    return pl.pallas_call(
        functools.partial(main_kernel, count, size),
        out_shape=(grad, grad, grad, share, share),
        in_specs=[any_spec] * 6 + [smem] * 3,
        out_specs=(any_spec, any_spec, any_spec, vmem, vmem),
        scratch_shapes=[
            pltpu.VMEM((4, SPOTS, CHANNELS), BF16),
            pltpu.VMEM((HEADS, 4, 256, DIM), BF16),
            pltpu.VMEM((HEADS, 3, 256, DIM), BF16),
            pltpu.VMEM((HEADS, 3, SPOTS, DIM), BF16),
            pltpu.VMEM((HEADS, 3, SPOTS, DIM), F32),
            pltpu.VMEM((3, SPOTS, CHANNELS), BF16),
            pltpu.VMEM((256, 256), F32),
            pltpu.VMEM((2 * HEADS, DIM), F32),
            pltpu.VMEM((2 * HEADS, DIM), F32),
            pltpu.VMEM((8, DIM), F32),
            pltpu.VMEM((8, DIM), F32),
            pltpu.VMEM((count, 8, DIM), F32),
            pltpu.VMEM((count, 8, DIM), F32),
            pltpu.VMEM((count, 8, DIM), F32),
            pltpu.VMEM((8, DIM), F32),
            pltpu.VMEM((FRAMES, 8, DIM), F32),
            pltpu.VMEM((2, 1, size), F32),
            pltpu.SemaphoreType.REGULAR((2,)),
            pltpu.SemaphoreType.DMA((2,)),
            pltpu.SemaphoreType.DMA((4,)),
            pltpu.SemaphoreType.DMA((HEADS,)),
            pltpu.SemaphoreType.DMA((HEADS,)),
            pltpu.SemaphoreType.DMA((HEADS,)),
            pltpu.SemaphoreType.DMA((HEADS,)),
            pltpu.SemaphoreType.DMA((HEADS,)),
            pltpu.SemaphoreType.DMA((3,)),
            pltpu.SemaphoreType.DMA((6,)),
        ],
        compiler_params=pltpu.CompilerParams(
            collective_id=1, has_side_effects=True, vmem_limit_bytes=40 << 20
        ),
        name="axial",
    )(*arrays)


def emit_kernel(*refs):
    half = len(refs) // 2
    sem = refs[-1]
    copies = [
        pltpu.make_async_copy(src, dst, sem.at[i])
        for i, (src, dst) in enumerate(zip(refs[:half], refs[half:-1]))
    ]
    for copy in copies:
        copy.start()
    for copy in copies:
        copy.wait()


def emit(arrays):
    any_spec = pl.BlockSpec(memory_space=pl.ANY)
    vmem = pl.BlockSpec(memory_space=pltpu.VMEM)
    return pl.pallas_call(
        emit_kernel,
        out_shape=tuple(jax.ShapeDtypeStruct(x.shape, x.dtype) for x in arrays),
        in_specs=[vmem] * len(arrays),
        out_specs=(any_spec,) * len(arrays),
        scratch_shapes=[pltpu.SemaphoreType.DMA((len(arrays),))],
        compiler_params=pltpu.CompilerParams(vmem_limit_bytes=8 << 20),
        name="emit",
    )(*arrays)


def shards(query_input, key_input, value_input, cotangent, q_gain, k_gain, frames, heights, widths):
    count = lax.axis_size("dp")
    flat = (SPOTS, CHANNELS)
    results = main_call(
        query_input.reshape(flat),
        key_input.reshape(flat),
        value_input.reshape(flat),
        cotangent.reshape(flat),
        q_gain,
        k_gain,
        frames,
        heights,
        widths,
        count,
    )
    query_grad, key_grad, value_grad, share_q, share_k = emit(results)
    full = (1, 1, SPOTS, CHANNELS)
    return (
        query_grad.reshape(full),
        key_grad.reshape(full),
        value_grad.reshape(full),
        share_q.reshape(-1),
        share_k.reshape(-1),
    )


def solution(mesh):
    tokens = P("dp", "seq", None, None)
    return jax.shard_map(
        shards,
        mesh=mesh,
        in_specs=(tokens,) * 4 + (P("dp"),) * 5,
        out_specs=(tokens,) * 3 + (P("dp"),) * 2,
        check_vma=False,
    )
```
